512 devices in a mesh: ctx: 64 (over y_lo, z, core), tp: 4 (over x), seq: 2 (over y_hi).
Axes of the slice: x: 4, y: 8 (y_hi: 2, y_lo: 4; y = y_hi * 4 + y_lo), z: 8, core: 2. Of those that a mesh axis runs over, the one named last changes fastest.
Arguments:
- queries: bfloat16 [2, 16384, 4096], P('seq', 'ctx', 'tp'), may hold values from -24 to 24
- attention_keys: bfloat16 [2, 16384, 512], P('seq', 'ctx', 'tp'), may hold values from -12 to 12
- attention_values: bfloat16 [2, 16384, 512], P('seq', 'ctx', 'tp'), may hold values from -6 to 6
- cotangent: bfloat16 [2, 16384, 4096], P('seq', 'ctx', 'tp'), may hold values from -6 to 6
- low_rank: bfloat16 [2, 16384, 128], P('seq', 'ctx'), may hold values from -22 to 22
- seq_lengths: int32 [2], replicated, may hold values from 8192 to 16384, as said below
- window_stops: int32 [2], replicated, may hold values from 128 to 768, as said below
- query_ids: int32 [512], replicated, may hold values from 0 to 511, each once
- query_up_gradients: float32 [512, 64, 4096], P('seq', 'ctx', 'tp'), may hold values from -6 to 6
- value_up_gradients: float32 [512, 64, 512], P('seq', 'ctx', 'tp'), may hold values from -6 to 6
Outputs:
- ranked: float32 [512, 2], replicated
The draws below stay inside these ranges and needn't reach their ends.
Inputs may be any that keep to these rules, and one draw needn't show every extreme that they name: `seq_lengths`: some sequence has exactly 16384, and some other one fewer. `window_stops`: some sequence has exactly 768.
All inputs are finite; a program needn't handle non-finite values.
Results may differ from the reference program's by a relative error of at most 0.0056.
Values may be sent and summed in bfloat16 or wider, within the bound.
No kernel may reach another device: no remote copies, remote signals or barrier semaphores. Data moves between devices by JAX's collectives and lax.ppermute only.
A program may use at most 64 MiB of HBM per device.

```python
import jax
import jax.numpy as jnp
from jax import lax

QUERY_HEADS = 32
KEY_VALUE_HEADS = 4
HEAD_SIZE = 128
ADAPTER_RANK = 64
WINDOW_BLOCKS = 3
DEVICE_TOKENS = 256
QUERY_GRAD_COUNT = 512
SEQUENCE_COUNT = 2
TOKEN_SLOTS = 16384


def shared_pair(key):
    base_q = jnp.clip(jax.random.normal(jax.random.fold_in(key, 11), (SEQUENCE_COUNT, TOKEN_SLOTS, QUERY_HEADS * HEAD_SIZE), jnp.float32), -6.0, 6.0)
    base_keys = jnp.clip(jax.random.normal(jax.random.fold_in(key, 12), (SEQUENCE_COUNT, TOKEN_SLOTS, KEY_VALUE_HEADS * HEAD_SIZE), jnp.float32), -6.0, 6.0)
    return (base_q, base_keys)


def draw_queries(key, part):
    base_q, base_keys = shared_pair(key)
    result = base_q
    return result.astype(jnp.bfloat16)


def draw_attention_keys(key, part):
    base_q, base_keys = shared_pair(key)
    result = base_keys
    return result.astype(jnp.bfloat16)


def draw_low_rank(key, part):
    key = jax.random.fold_in(key, 5)
    column = (jnp.arange(2 * ADAPTER_RANK) % ADAPTER_RANK).astype(jnp.float32)
    jitter = jnp.exp(jax.random.uniform(jax.random.fold_in(key, 1), (2 * ADAPTER_RANK,), jnp.float32, -0.22, 0.22))
    spread = 3.0 ** (column / ADAPTER_RANK)
    values = jnp.clip(jax.random.normal(jax.random.fold_in(key, 2), (SEQUENCE_COUNT, TOKEN_SLOTS, 2 * ADAPTER_RANK), jnp.float32), -4.0, 4.0)
    return (values * spread * jitter).astype(jnp.bfloat16)


def draw_seq_lengths(key, part):
    key = jax.random.fold_in(key, 21)
    values = jax.random.randint(jax.random.fold_in(key, 1), (SEQUENCE_COUNT,), TOKEN_SLOTS // 2, TOKEN_SLOTS + 1)
    shorter = jax.random.randint(jax.random.fold_in(key, 3), (SEQUENCE_COUNT,), TOKEN_SLOTS // 2, TOKEN_SLOTS)
    longest = jax.random.randint(jax.random.fold_in(key, 2), (), 0, SEQUENCE_COUNT)
    index_list = jnp.arange(SEQUENCE_COUNT)
    follower = (longest + 1) % SEQUENCE_COUNT
    values = jnp.where(index_list == follower, shorter, values)
    return jnp.where(index_list == longest, TOKEN_SLOTS, values).astype(jnp.int32)


def draw_window_stops(key, part):
    key = jax.random.fold_in(key, 31)
    widest_value = WINDOW_BLOCKS * DEVICE_TOKENS
    values = jax.random.randint(jax.random.fold_in(key, 1), (SEQUENCE_COUNT,), DEVICE_TOKENS // 2, widest_value + 1)
    widest = jax.random.randint(jax.random.fold_in(key, 2), (), 0, SEQUENCE_COUNT)
    index_list = jnp.arange(SEQUENCE_COUNT)
    return jnp.where(index_list == widest, widest_value, values).astype(jnp.int32)


def shard_levels(stream_key, dims, shards, low, top_value):
    loudness = 1.0
    for dim, parts in shards:
        steps = jax.random.uniform(jax.random.fold_in(jax.random.fold_in(stream_key, 6), dim), (parts,), jnp.float32, low / len(shards), top_value / len(shards))
        loudness = loudness * jnp.repeat(jnp.exp(steps), dims[dim] // parts).reshape((-1,) + (1,) * (len(dims) - 1 - dim))
    return loudness


def gaussian(stream_key, extent, deviation, bound, pieces=(), kind=jnp.bfloat16):
    array = jax.random.normal(stream_key, extent, jnp.float32) * deviation
    if len(pieces) > 0:
        array = shard_levels(stream_key, extent, pieces, -0.22, 0.18) * array
    return jnp.clip(array, min=-bound, max=bound).astype(kind)


def setup_inputs(seed: int = 0) -> dict:
    keys = jax.random.split(jax.random.key(seed), 11)
    queries = draw_queries(jax.random.fold_in(keys[10], 71), 0)
    attention_keys = draw_attention_keys(jax.random.fold_in(keys[10], 71), 0)
    attention_values = gaussian(keys[2], (SEQUENCE_COUNT, TOKEN_SLOTS, KEY_VALUE_HEADS * HEAD_SIZE), 1.0, 6.0, ((0, 2), (1, 64), (2, 4)))
    cotangent = gaussian(keys[3], (SEQUENCE_COUNT, TOKEN_SLOTS, QUERY_HEADS * HEAD_SIZE), 1.0, 6.0, ((0, 2), (1, 64), (2, 4)))
    low_rank = draw_low_rank(jax.random.fold_in(keys[10], 71), 0)
    seq_lengths = draw_seq_lengths(jax.random.fold_in(keys[10], 71), 0)
    window_stops = draw_window_stops(jax.random.fold_in(keys[10], 71), 0)
    query_ids = jax.random.permutation(keys[7], QUERY_GRAD_COUNT).astype(jnp.int32)
    query_up_gradients = gaussian(keys[8], (QUERY_GRAD_COUNT, ADAPTER_RANK, QUERY_HEADS * HEAD_SIZE), 1.0, 6.0, ((0, 2), (1, 64), (2, 4)), jnp.float32)
    value_up_gradients = gaussian(keys[9], (QUERY_GRAD_COUNT, ADAPTER_RANK, KEY_VALUE_HEADS * HEAD_SIZE), 1.0, 6.0, ((0, 2), (1, 64), (2, 4)), jnp.float32)
    return {"queries": queries, "attention_keys": attention_keys, "attention_values": attention_values, "cotangent": cotangent, "low_rank": low_rank, "seq_lengths": seq_lengths, "window_stops": window_stops, "query_ids": query_ids, "query_up_gradients": query_up_gradients, "value_up_gradients": value_up_gradients}


NEG_FILL = -1e+30

def sequence_grads(queries, attention_keys, attention_values, cotangent, length, reach):
    head_group = QUERY_HEADS // KEY_VALUE_HEADS
    scale_factor = HEAD_SIZE ** (-0.5)
    block_list = TOKEN_SLOTS // DEVICE_TOKENS
    span = (WINDOW_BLOCKS + 1) * DEVICE_TOKENS
    positions = jnp.arange(TOKEN_SLOTS, dtype=jnp.int32)
    output_gradient = jnp.where((positions < length)[:, None], cotangent, jnp.zeros_like(cotangent))
    query_total = queries.reshape(TOKEN_SLOTS, KEY_VALUE_HEADS, head_group, HEAD_SIZE)
    gradient_total = output_gradient.reshape(TOKEN_SLOTS, KEY_VALUE_HEADS, head_group, HEAD_SIZE)
    leading_part = jnp.zeros((WINDOW_BLOCKS * DEVICE_TOKENS, KEY_VALUE_HEADS * HEAD_SIZE), attention_keys.dtype)
    key_padding = jnp.concatenate([leading_part, attention_keys], axis=0).reshape(-1, KEY_VALUE_HEADS, HEAD_SIZE)
    value_padding = jnp.concatenate([leading_part, attention_values], axis=0).reshape(-1, KEY_VALUE_HEADS, HEAD_SIZE)
    offsets = jnp.arange(DEVICE_TOKENS, dtype=jnp.int32)
    key_offsets = jnp.arange(span, dtype=jnp.int32)

    def one_block(block):
        start = (block * DEVICE_TOKENS).astype(jnp.int32)
        query_block = lax.dynamic_slice_in_dim(query_total, start, DEVICE_TOKENS, 0).astype(jnp.float32)
        grad_block = lax.dynamic_slice_in_dim(gradient_total, start, DEVICE_TOKENS, 0).astype(jnp.float32)
        key_block = lax.dynamic_slice_in_dim(key_padding, start, span, 0).astype(jnp.float32)
        value_block = lax.dynamic_slice_in_dim(value_padding, start, span, 0).astype(jnp.float32)
        query_pos = start + offsets
        key_pos = start - WINDOW_BLOCKS * DEVICE_TOKENS + key_offsets
        gap = query_pos[:, None] - key_pos[None, :]
        allowed = (gap >= 0) & (gap < reach) & (key_pos[None, :] < length) & (key_pos[None, :] >= 0)
        scores = jnp.einsum('qhgd,khd->hgqk', query_block, key_block) * scale_factor
        scores = jnp.where(allowed, scores, NEG_FILL)
        top = lax.optimization_barrier(jnp.max(scores, axis=-1))
        log_total = top + jnp.log(lax.optimization_barrier(jnp.sum(jnp.exp(scores - top[..., None]), axis=-1)))
        prob = jnp.exp(scores - log_total[..., None])
        dprob = jnp.einsum('qhgd,khd->hgqk', grad_block, value_block)
        inner = lax.optimization_barrier(jnp.sum(prob * dprob, axis=-1))
        dscore = lax.optimization_barrier((prob * (dprob - inner[..., None])).astype(jnp.bfloat16)).astype(jnp.float32)
        query_gradient = (jnp.einsum('hgqk,khd->qhgd', dscore, key_block) * scale_factor).astype(jnp.bfloat16)
        prob_round = lax.optimization_barrier(prob.astype(jnp.bfloat16)).astype(jnp.float32)
        value_portion = jnp.einsum('hgqk,qhgd->khd', prob_round, grad_block)
        return (query_gradient.reshape(DEVICE_TOKENS, QUERY_HEADS * HEAD_SIZE), value_portion.reshape(WINDOW_BLOCKS + 1, DEVICE_TOKENS, KEY_VALUE_HEADS * HEAD_SIZE))
    query_grads, value_parts = lax.map(one_block, jnp.arange(block_list, dtype=jnp.int32))
    query_gradient = query_grads.reshape(TOKEN_SLOTS, QUERY_HEADS * HEAD_SIZE)
    trailing_part = jnp.zeros((WINDOW_BLOCKS, DEVICE_TOKENS, KEY_VALUE_HEADS * HEAD_SIZE), jnp.float32)
    value_total = jnp.zeros((block_list, DEVICE_TOKENS, KEY_VALUE_HEADS * HEAD_SIZE), jnp.float32)
    for slot in range(WINDOW_BLOCKS + 1):
        padded = jnp.concatenate([value_parts[:, slot], trailing_part], axis=0)
        value_total = value_total + padded[WINDOW_BLOCKS - slot:WINDOW_BLOCKS - slot + block_list]
    value_gradient = value_total.reshape(TOKEN_SLOTS, KEY_VALUE_HEADS * HEAD_SIZE).astype(jnp.bfloat16)
    return (query_gradient, value_gradient)

def reference(queries, attention_keys, attention_values, cotangent, low_rank, seq_lengths, window_stops, query_ids, query_up_gradients, value_up_gradients):
    columns = []
    for sequence in range(SEQUENCE_COUNT):
        query_gradient, value_gradient = sequence_grads(queries[sequence], attention_keys[sequence], attention_values[sequence], cotangent[sequence], seq_lengths[sequence], window_stops[sequence])
        query_down_weight = low_rank[sequence, :, :ADAPTER_RANK].astype(jnp.float32)
        value_down_weight = low_rank[sequence, :, ADAPTER_RANK:].astype(jnp.float32)
        query_adapter = jnp.einsum('gz,gs->zs', query_down_weight, query_gradient.astype(jnp.float32), precision=lax.Precision.HIGHEST)
        value_adapter = jnp.einsum('gz,gs->zs', value_down_weight, value_gradient.astype(jnp.float32), precision=lax.Precision.HIGHEST)
        gradient_norm_value = jnp.sqrt(jnp.sum(query_adapter * query_adapter) + jnp.sum(value_adapter * value_adapter) + 1e-06)
        score_value = jnp.einsum('ujb,jb->u', query_up_gradients, query_adapter, precision=lax.Precision.HIGHEST)
        score_value = score_value + jnp.einsum('ujb,jb->u', value_up_gradients, value_adapter, precision=lax.Precision.HIGHEST)
        columns.append(score_value / gradient_norm_value)
    scores_all = jnp.stack(columns, axis=1)
    return scores_all[query_ids]
```

```python
import functools

import jax
import jax.numpy as jnp
from jax import lax
from jax.experimental import pallas as pl
from jax.experimental.pallas import tpu as pltpu
from jax.sharding import Mesh
from jax.sharding import PartitionSpec as P

HEAD_SIZE = 128
WINDOW_BLOCKS = 3
TOKENS = 256
RANK = 64
HEADS = 8
KEYS = (WINDOW_BLOCKS + 1) * TOKENS
FEATURES = HEADS * HEAD_SIZE + HEAD_SIZE
SHARE = 256
LINE = 2 * SHARE + 128
NEG_FILL = -1e30
SCALE = HEAD_SIZE ** (-0.5)
LOG2E = 1.4426950408889634

CTX = ("y", "z", "core")
VMEM = pl.BlockSpec(memory_space=pltpu.VMEM)
SMEM = pl.BlockSpec(memory_space=pltpu.SMEM)
NT = (((1,), (1,)), ((), ()))


def passed_along(x, by):
    peers = 64
    return lax.ppermute(x, CTX, [(i, i + by) for i in range(peers - by)])


def attention_kernel(
    place, lengths, stops, q_ref, g_ref, low_ref, pack0, pack1, pack2, pack3,
    out_ref, keys, values, keys_t, low_t, bias, sums,
):
    ctx = place[0]
    seq = place[1]
    length = lengths[seq]
    reach = stops[seq]
    for stop, pack in enumerate((pack0, pack1, pack2, pack3)):
        rows = pl.ds(stop * TOKENS, TOKENS)
        key_block = pack[0:TOKENS, :]
        keys[rows, :] = key_block
        values[rows, :] = pack[TOKENS : 2 * TOKENS, :]
        keys_t[:, rows] = key_block.T
        low_pair = pack[2 * TOKENS : 2 * TOKENS + 128, :].T
        low_t[:, stop * TOKENS : stop * TOKENS + 128] = low_pair[:RANK]
        low_t[:, stop * TOKENS + 128 : (stop + 1) * TOKENS] = low_pair[RANK:]
        row = lax.broadcasted_iota(jnp.int32, (TOKENS, TOKENS), 0)
        col = lax.broadcasted_iota(jnp.int32, (TOKENS, TOKENS), 1)
        gap = col - row + stop * TOKENS
        key_pos = (ctx - stop) * TOKENS + row
        allowed = (gap >= 0) & (gap < reach) & (key_pos < length) & (key_pos >= 0)
        bias[rows, :] = jnp.where(allowed, 0.0, NEG_FILL)
    query_low = low_ref[...].T[:RANK]
    token = lax.broadcasted_iota(jnp.int32, (TOKENS, HEAD_SIZE), 0)
    live = jnp.where(ctx * TOKENS + token < length, 1.0, 0.0).astype(jnp.bfloat16)
    value_sum = jnp.zeros((KEYS, HEAD_SIZE), jnp.float32)
    for head in range(HEADS):
        lanes = slice(head * HEAD_SIZE, (head + 1) * HEAD_SIZE)
        q = q_ref[:, lanes]
        g = g_ref[:, lanes] * live
        scores = lax.dot_general(keys[...], q, NT, preferred_element_type=jnp.float32)
        scores = scores * (SCALE * LOG2E) + bias[...]
        dprob = lax.dot_general(values[...], g, NT, preferred_element_type=jnp.float32)
        top = jnp.max(scores, axis=0, keepdims=True)
        weights = jnp.exp2(scores - top)
        fraction = 1.0 / jnp.sum(weights, axis=0, keepdims=True)
        inner = jnp.sum(weights * dprob, axis=0, keepdims=True) * fraction
        prob = weights * fraction
        dscore = (prob * (dprob - inner)).astype(jnp.bfloat16)
        query_grad = jnp.dot(keys_t[...], dscore, preferred_element_type=jnp.float32)
        query_grad = (query_grad * SCALE).astype(jnp.bfloat16)
        sums[head] = lax.dot_general(
            query_low, query_grad, NT, preferred_element_type=jnp.float32
        )
        value_sum = value_sum + jnp.dot(
            prob.astype(jnp.bfloat16), g, preferred_element_type=jnp.float32
        )
    sums[HEADS] = jnp.dot(
        low_t[...], value_sum.astype(jnp.bfloat16), preferred_element_type=jnp.float32
    )
    for head in range(HEADS + 1):
        lanes = slice(head * HEAD_SIZE, (head + 1) * HEAD_SIZE)
        out_ref[0:32, lanes] = sums[head, pl.ds(0, 32, stride=2), :]
        out_ref[32:64, lanes] = sums[head, pl.ds(1, 32, stride=2), :]


def pair_kernel(in_ref, out_ref):
    total = in_ref[0:32, :] + in_ref[32:64, :]
    out_ref[0:32, 0, :] = total
    out_ref[32:64, 0, :] = total


def score_kernel(rows_ref, up_query, up_value, out_ref):
    pieces = []
    squares = []
    for b in range(2):
        row = jnp.sum(rows_ref[b * 32 : (b + 1) * 32, :, :], axis=0)
        squares.append(jnp.sum(row * row))
        total = up_value[...] * row[:, HEADS * HEAD_SIZE :]
        for k in range(HEADS):
            total = total + up_query[pl.ds(k, SHARE, stride=HEADS), :] * row[
                :, k * HEAD_SIZE : (k + 1) * HEAD_SIZE
            ]
        pieces.append(jnp.sum(total.T, axis=0, keepdims=True))
    lane = lax.broadcasted_iota(jnp.int32, (1, 128), 1)
    tail = jnp.where(lane == 0, squares[0], jnp.where(lane == 1, squares[1], 0.0))
    line = jnp.concatenate(pieces + [tail], axis=1)
    for i in range(out_ref.shape[0]):
        out_ref[i] = line


def relay_kernel(in_ref, out_ref):
    line = jnp.sum(in_ref[...], axis=0)
    for i in range(out_ref.shape[0]):
        out_ref[i] = line


def final_kernel(in_ref, ids_ref, out_ref):
    halves = [jnp.sum(in_ref[s * 32 : (s + 1) * 32, :, :], axis=0) for s in range(2)]
    count = 2 * SHARE
    rest = []
    for b in range(2):
        square = halves[0][:, count + b : count + b + 1]
        part = [half[:, b * SHARE : (b + 1) * SHARE] for half in halves]
        scores = jnp.concatenate(part, axis=1) / jnp.sqrt(square + 1e-06)
        rest.append(scores)
    slot = lax.broadcasted_iota(jnp.int32, (count, count), 0)
    chosen = jnp.where(slot == ids_ref[...], 1.0, 0.0).astype(jnp.bfloat16)
    stack = jnp.concatenate(rest + [jnp.zeros((6, count), jnp.float32)], axis=0)
    total = jnp.zeros((8, count), jnp.float32)
    for _ in range(3):
        piece = stack.astype(jnp.bfloat16)
        stack = stack - piece.astype(jnp.float32)
        total = total + jnp.dot(piece, chosen, preferred_element_type=jnp.float32)
    out_ref[...] = total[0:2]


def call(kernel, shape, dtype, specs, scratch=(), flops=0):
    return pl.pallas_call(
        kernel,
        out_shape=jax.ShapeDtypeStruct(shape, dtype),
        in_specs=specs,
        out_specs=VMEM,
        scratch_shapes=list(scratch),
        compiler_params=pltpu.CompilerParams(vmem_limit_bytes=24 * 2**20),
        cost_estimate=pl.CostEstimate(flops=flops, bytes_accessed=2**20, transcendentals=0),
    )


def body(
    queries, attention_keys, attention_values, cotangent, low_rank, seq_lengths,
    window_stops, query_ids, query_up_gradients, value_up_gradients,
):
    low = low_rank[0]
    pack = jnp.concatenate(
        [
            attention_keys[0],
            attention_values[0],
            jnp.concatenate([low[:128, RANK:], low[128:, RANK:]], axis=1),
        ],
        axis=0,
    )
    arrived = [passed_along(pack, by) for by in (1, 2, 3)]
    place = jnp.stack([lax.axis_index(CTX), lax.axis_index("seq")]).astype(jnp.int32)
    bf, f32 = jnp.bfloat16, jnp.float32
    sums = call(
        attention_kernel, (RANK, FEATURES), f32, [SMEM] * 3 + [VMEM] * 7,
        [
            pltpu.VMEM((KEYS, HEAD_SIZE), bf),
            pltpu.VMEM((KEYS, HEAD_SIZE), bf),
            pltpu.VMEM((HEAD_SIZE, KEYS), bf),
            pltpu.VMEM((RANK, KEYS), bf),
            pltpu.VMEM((KEYS, TOKENS), f32),
            pltpu.VMEM((HEADS + 1, RANK, HEAD_SIZE), f32),
        ],
        flops=2 * 4 * HEADS * TOKENS * KEYS * HEAD_SIZE,
    )(place, seq_lengths, window_stops, queries[0], cotangent[0], low, pack, *arrived)
    sums = lax.all_to_all(sums, "core", 0, 0, tiled=True)
    sums = call(pair_kernel, (RANK, 1, FEATURES), f32, [VMEM])(sums)
    sums = lax.all_to_all(sums, ("seq", "y", "z"), 0, 0, tiled=True)
    up_query = query_up_gradients.reshape(SHARE * HEADS, HEAD_SIZE)
    up_value = value_up_gradients.reshape(SHARE, HEAD_SIZE)
    lines = call(score_kernel, (8, 1, LINE), f32, [VMEM] * 3)(sums, up_query, up_value)
    lines = lax.all_to_all(lines, ("tp", "core"), 0, 0, tiled=True)
    lines = call(relay_kernel, (64, 1, LINE), f32, [VMEM])(lines)
    lines = lax.all_to_all(lines, ("seq", "y", "z"), 0, 0, tiled=True)
    ranked = call(final_kernel, (2, 2 * SHARE), f32, [VMEM] * 2)(
        lines, query_ids.reshape(1, 2 * SHARE)
    )
    return ranked.T


def solution(mesh):
    fine = Mesh(mesh.devices.reshape(4, 8, 2, 4, 2), ("y", "z", "core", "tp", "seq"))
    split = P("seq", CTX, "tp")
    placed = (split, split, split, split, P("seq", CTX, None), P(), P(), P(), split, split)
    return jax.shard_map(body, mesh=fine, in_specs=placed, out_specs=P(), check_vma=False)
```

```python
import functools

import jax
import jax.numpy as jnp
from jax import lax
from jax.experimental import pallas as pl
from jax.experimental.pallas import tpu as pltpu
from jax.sharding import Mesh
from jax.sharding import PartitionSpec as P

HEAD_SIZE = 128
WINDOW_BLOCKS = 3
TOKENS = 256
RANK = 64
HEADS = 8
KEYS = (WINDOW_BLOCKS + 1) * TOKENS
FEATURES = HEADS * HEAD_SIZE + HEAD_SIZE
HALF = 640
CHUNK = 64
CHUNKS = [slice(i * CHUNK, (i + 1) * CHUNK) for i in range(KEYS // CHUNK)]
EARLY = 2
SHARE = 256
LINE = 2 * SHARE + 128
NEG_FILL = -1e30
SCALE = HEAD_SIZE ** (-0.5)
LOG2E = 1.4426950408889634

CTX = ("y", "z", "core")
VMEM = pl.BlockSpec(memory_space=pltpu.VMEM)
SMEM = pl.BlockSpec(memory_space=pltpu.SMEM)
NT = (((1,), (1,)), ((), ()))


def lanes(head):
    return slice(head * HEAD_SIZE, (head + 1) * HEAD_SIZE)


def folded(x):
    return x.reshape(x.shape[0] // 8, 8, TOKENS)


def visible_bias(place, stop):
    row = lax.broadcasted_iota(jnp.int32, (TOKENS, TOKENS), 0)
    col = lax.broadcasted_iota(jnp.int32, (TOKENS, TOKENS), 1)
    gap = col - row + stop * TOKENS
    key_pos = (place[0] - stop) * TOKENS + row
    allowed = (gap >= 0) & (gap < place[2]) & (key_pos < place[1]) & (key_pos >= 0)
    return jnp.where(allowed, 0.0, NEG_FILL)


def live_rows(place):
    token = lax.broadcasted_iota(jnp.int32, (TOKENS, HEAD_SIZE), 0)
    live = place[0] * TOKENS + token < place[1]
    return jnp.where(live, 1.0, 0.0).astype(jnp.bfloat16)


def block_kernel(
    stop, place, queries, cotangent, pack, weight_ref, dprob_ref, stat_ref, bias, score_buf
):
    bias[...] = visible_bias(place, stop)
    live = live_rows(place)

    def products(head):
        score_buf[head % 2] = lax.dot_general(
            pack[0:TOKENS, :], queries[:, lanes(head)], NT, preferred_element_type=jnp.float32
        )
        dprob_ref[head] = lax.dot_general(
            pack[TOKENS : 2 * TOKENS, :],
            cotangent[:, lanes(head)] * live,
            NT,
            preferred_element_type=jnp.float32,
        )

    products(0)
    for head in range(HEADS):
        if head + 1 < HEADS:
            products(head + 1)
        side = head % 2
        top = jnp.full((8, TOKENS), -3e38, jnp.float32)
        for rows in CHUNKS[: TOKENS // CHUNK]:
            scores = score_buf[side, rows] * (SCALE * LOG2E) + bias[rows]
            score_buf[side, rows] = scores
            top = jnp.maximum(top, jnp.max(folded(scores), axis=0))
        top = jnp.max(top, axis=0, keepdims=True)
        total = jnp.zeros((8, TOKENS), jnp.float32)
        inner = jnp.zeros((8, TOKENS), jnp.float32)
        for rows in CHUNKS[: TOKENS // CHUNK]:
            weights = jnp.exp2(score_buf[side, rows] - top)
            weight_ref[head, rows] = weights
            total = total + jnp.sum(folded(weights), axis=0)
            inner = inner + jnp.sum(folded(weights * dprob_ref[head, rows]), axis=0)
        stat_ref[head, 0:1, :] = top
        stat_ref[head, 1:2, :] = jnp.sum(total, axis=0, keepdims=True)
        stat_ref[head, 2:3, :] = jnp.sum(inner, axis=0, keepdims=True)


def attention_kernel(early_count, *refs):
    place, queries, cotangent, low_ref = refs[:4]
    packs = refs[4:8]
    early = [refs[8 + 3 * i : 11 + 3 * i] for i in range(early_count)]
    (
        out_ref, keys, values, keys_t, low_t, bias, sums,
        score_buf, dprob_buf, prob_buf, dscore_buf,
    ) = refs[8 + 3 * early_count :]
    near = 1 + 2 * (place[0] % 2)
    stops = (0, 2, near, 4 - near)
    for slot in range(WINDOW_BLOCKS + 1):
        pack = packs[slot]
        rows = pl.ds(slot * TOKENS, TOKENS)
        key_block = pack[0:TOKENS, :]
        if slot >= early_count:
            fresh = pl.ds((slot - early_count) * TOKENS, TOKENS)
            keys[fresh, :] = key_block
            values[fresh, :] = pack[TOKENS : 2 * TOKENS, :]
            bias[fresh, :] = visible_bias(place, stops[slot])
        keys_t[:, rows] = key_block.T
        low_pair = pack[2 * TOKENS : 2 * TOKENS + 128, :].T
        low_t[:, slot * TOKENS : slot * TOKENS + 128] = low_pair[:RANK]
        low_t[:, slot * TOKENS + 128 : (slot + 1) * TOKENS] = low_pair[RANK:]
    query_low = low_ref[...].T[:RANK]
    live = live_rows(place)
    offset = early_count * TOKENS
    fresh_chunks = CHUNKS[: (KEYS - offset) // CHUNK]

    def products(head):
        side = head % 2
        score_buf[side] = lax.dot_general(
            keys[...], queries[:, lanes(head)], NT, preferred_element_type=jnp.float32
        )
        dprob_buf[side] = lax.dot_general(
            values[...], cotangent[:, lanes(head)] * live, NT, preferred_element_type=jnp.float32
        )

    def softmax(head):
        side = head % 2
        top = jnp.full((8, TOKENS), -3e38, jnp.float32)
        for rows in fresh_chunks:
            scores = score_buf[side, rows] * (SCALE * LOG2E) + bias[rows]
            score_buf[side, rows] = scores
            top = jnp.maximum(top, jnp.max(folded(scores), axis=0))
        top = jnp.max(top, axis=0, keepdims=True)
        for _, _, stat in early:
            top = jnp.maximum(top, stat[head, 0:1, :])
        total = jnp.zeros((8, TOKENS), jnp.float32)
        inner = jnp.zeros((8, TOKENS), jnp.float32)
        for rows in fresh_chunks:
            weights = jnp.exp2(score_buf[side, rows] - top)
            score_buf[side, rows] = weights
            total = total + jnp.sum(folded(weights), axis=0)
            inner = inner + jnp.sum(folded(weights * dprob_buf[side, rows]), axis=0)
        total = jnp.sum(total, axis=0, keepdims=True)
        inner = jnp.sum(inner, axis=0, keepdims=True)
        fades = []
        for _, _, stat in early:
            fade = jnp.exp2(stat[head, 0:1, :] - top)
            total = total + fade * stat[head, 1:2, :]
            inner = inner + fade * stat[head, 2:3, :]
            fades.append(fade)
        fraction = 1.0 / total
        inner = inner * fraction

        def settle(weights, dprob, factor, at):
            prob = weights * factor
            prob_buf[side, at : at + CHUNK] = prob.astype(jnp.bfloat16)
            dscore_buf[side, at : at + CHUNK] = (prob * (dprob - inner)).astype(jnp.bfloat16)

        for slot, (weight, dprob, _) in enumerate(early):
            factor = fades[slot] * fraction
            for rows in CHUNKS[: TOKENS // CHUNK]:
                settle(weight[head, rows], dprob[head, rows], factor, slot * TOKENS + rows.start)
        for rows in fresh_chunks:
            settle(score_buf[side, rows], dprob_buf[side, rows], fraction, offset + rows.start)

    def finish(head, value_sum):
        side = head % 2
        query_grad = jnp.dot(keys_t[...], dscore_buf[side], preferred_element_type=jnp.float32)
        query_grad = (query_grad * SCALE).astype(jnp.bfloat16)
        sums[head] = lax.dot_general(
            query_low, query_grad, NT, preferred_element_type=jnp.float32
        )
        g = cotangent[:, lanes(head)] * live
        return value_sum + jnp.dot(prob_buf[side], g, preferred_element_type=jnp.float32)

    value_sum = jnp.zeros((KEYS, HEAD_SIZE), jnp.float32)
    products(0)
    for head in range(HEADS):
        if head + 1 < HEADS:
            products(head + 1)
        if head > 0:
            value_sum = finish(head - 1, value_sum)
        softmax(head)
    value_sum = finish(HEADS - 1, value_sum)
    sums[HEADS] = jnp.dot(
        low_t[...], value_sum.astype(jnp.bfloat16), preferred_element_type=jnp.float32
    )
    for head in range(HEADS + 1):
        out_ref[0:32, lanes(head)] = sums[head, pl.ds(0, 32, stride=2), :]
        out_ref[32:64, lanes(head)] = sums[head, pl.ds(1, 32, stride=2), :]


def pair_kernel(in_ref, out_ref):
    total = in_ref[0:32, :] + in_ref[32:64, :]
    upper = jnp.concatenate([total[:, HALF:], jnp.zeros((32, 2 * HALF - FEATURES))], axis=1)
    both = jnp.stack([total[:, :HALF], upper], axis=1).astype(jnp.bfloat16)
    out_ref[0:32] = both
    out_ref[32:64] = both


def score_kernel(rows_ref, up_query, up_value, out_ref):
    pieces = []
    squares = []
    for b in range(2):
        row = jnp.sum(rows_ref[b * 32 : (b + 1) * 32].astype(jnp.float32), axis=0)
        row = jnp.concatenate([row[0:1], row[1:2, : FEATURES - HALF]], axis=1)
        squares.append(jnp.sum(row * row))
        total = up_value[...] * row[:, HEADS * HEAD_SIZE :]
        for k in range(HEADS):
            total = total + up_query[pl.ds(k, SHARE, stride=HEADS), :] * row[
                :, k * HEAD_SIZE : (k + 1) * HEAD_SIZE
            ]
        pieces.append(jnp.sum(total.T, axis=0, keepdims=True))
    lane = lax.broadcasted_iota(jnp.int32, (1, 128), 1)
    tail = jnp.where(lane == 0, squares[0], jnp.where(lane == 1, squares[1], 0.0))
    line = jnp.concatenate(pieces + [tail], axis=1)
    for i in range(out_ref.shape[0]):
        out_ref[i] = line


def relay_kernel(in_ref, out_ref):
    line = jnp.sum(in_ref[...], axis=0)
    for i in range(out_ref.shape[0]):
        out_ref[i] = line


def final_kernel(in_ref, ids_ref, out_ref):
    halves = [jnp.sum(in_ref[s * 32 : (s + 1) * 32, :, :], axis=0) for s in range(2)]
    count = 2 * SHARE
    rest = []
    for b in range(2):
        square = halves[0][:, count + b : count + b + 1]
        part = [half[:, b * SHARE : (b + 1) * SHARE] for half in halves]
        scores = jnp.concatenate(part, axis=1) / jnp.sqrt(square + 1e-06)
        rest.append(scores)
    slot = lax.broadcasted_iota(jnp.int32, (count, count), 0)
    chosen = jnp.where(slot == ids_ref[...], 1.0, 0.0).astype(jnp.bfloat16)
    left = jnp.concatenate(rest, axis=0)
    pieces = []
    for _ in range(3):
        piece = left.astype(jnp.bfloat16)
        left = left - piece.astype(jnp.float32)
        pieces.append(piece.astype(jnp.float32))
    pieces.append(jnp.zeros((2, count), jnp.float32))
    stack = jnp.concatenate(pieces, axis=0).astype(jnp.bfloat16)
    total = jnp.dot(stack, chosen, preferred_element_type=jnp.float32)
    out_ref[...] = total[0:2] + total[2:4] + total[4:6]


def call(kernel, shape, dtype, specs, scratch=(), flops=0):
    many = isinstance(shape, list)
    made = [jax.ShapeDtypeStruct(dims, dtype) for dims in (shape if many else [shape])]
    return pl.pallas_call(
        kernel,
        out_shape=made if many else made[0],
        in_specs=specs,
        out_specs=[VMEM] * len(made) if many else VMEM,
        scratch_shapes=list(scratch),
        compiler_params=pltpu.CompilerParams(vmem_limit_bytes=32 * 2**20),
        cost_estimate=pl.CostEstimate(flops=flops, bytes_accessed=2**20, transcendentals=0),
    )


def body(
    queries, attention_keys, attention_values, cotangent, low_rank, seq_lengths,
    window_stops, query_ids, query_up_gradients, value_up_gradients,
):
    low = low_rank[0]
    pack = jnp.concatenate(
        [
            attention_keys[0],
            attention_values[0],
            jnp.concatenate([low[:128, RANK:], low[128:, RANK:]], axis=1),
        ],
        axis=0,
    )
    count = 64
    early = lax.ppermute(pack, CTX, [(i, i + 2) for i in range(count - 2)])
    apart = [(i, i + 1 + 2 * (i % 2)) for i in range(count) if i + 1 + 2 * (i % 2) < count]
    far = lax.ppermute(pack, CTX, apart)
    second = lax.axis_index("seq") == 1
    place = jnp.stack(
        [
            lax.axis_index(CTX).astype(jnp.int32),
            jnp.where(second, seq_lengths[1], seq_lengths[0]),
            jnp.where(second, window_stops[1], window_stops[0]),
        ]
    )
    bf, f32 = jnp.bfloat16, jnp.float32
    tile = (TOKENS, TOKENS)

    def block(stop, block_pack):
        return call(
            functools.partial(block_kernel, stop),
            [(HEADS, *tile), (HEADS, *tile), (HEADS, 8, TOKENS)], f32, [SMEM] + [VMEM] * 3,
            [pltpu.VMEM(tile, f32), pltpu.VMEM((2, *tile), f32)],
            flops=2 * 2 * HEADS * TOKENS * TOKENS * HEAD_SIZE,
        )(place, queries[0], cotangent[0], block_pack)

    ready = list(block(0, pack))
    early, ready[2] = lax.optimization_barrier((early, ready[2]))
    other = lax.ppermute(early, "core", [(0, 1), (1, 0)])
    ready += list(block(2, early))
    packs = [pack, early, other, far]
    fresh = KEYS - EARLY * TOKENS
    sums = call(
        functools.partial(attention_kernel, EARLY), (RANK, FEATURES), f32,
        [SMEM] + [VMEM] * (7 + 3 * EARLY),
        [
            pltpu.VMEM((fresh, HEAD_SIZE), bf),
            pltpu.VMEM((fresh, HEAD_SIZE), bf),
            pltpu.VMEM((HEAD_SIZE, KEYS), bf),
            pltpu.VMEM((RANK, KEYS), bf),
            pltpu.VMEM((fresh, TOKENS), f32),
            pltpu.VMEM((HEADS + 1, RANK, HEAD_SIZE), f32),
            pltpu.VMEM((2, fresh, TOKENS), f32),
            pltpu.VMEM((2, fresh, TOKENS), f32),
            pltpu.VMEM((2, KEYS, TOKENS), bf),
            pltpu.VMEM((2, KEYS, TOKENS), bf),
        ],
        flops=2 * 4 * HEADS * TOKENS * KEYS * HEAD_SIZE,
    )(place, queries[0], cotangent[0], low, *packs, *ready)
    sums = lax.all_to_all(sums, "core", 0, 0, tiled=True)
    sums = call(pair_kernel, (RANK, 2, HALF), bf, [VMEM])(sums)
    sums = lax.all_to_all(sums, ("seq", "y", "z"), 0, 0, tiled=True)
    up_query = query_up_gradients.reshape(SHARE * HEADS, HEAD_SIZE)
    up_value = value_up_gradients.reshape(SHARE, HEAD_SIZE)
    lines = call(score_kernel, (8, 1, LINE), f32, [VMEM] * 3)(sums, up_query, up_value)
    lines = lax.all_to_all(lines, ("tp", "core"), 0, 0, tiled=True)
    lines = call(relay_kernel, (64, 1, LINE), f32, [VMEM])(lines)
    lines = lax.all_to_all(lines, ("seq", "y", "z"), 0, 0, tiled=True)
    ranked = call(final_kernel, (2, 2 * SHARE), f32, [VMEM] * 2)(
        lines, query_ids.reshape(1, 2 * SHARE)
    )
    return ranked.T


def solution(mesh):
    fine = Mesh(mesh.devices.reshape(4, 8, 2, 4, 2), ("y", "z", "core", "tp", "seq"))
    split = P("seq", CTX, "tp")
    placed = (split, split, split, split, P("seq", CTX, None), P(), P(), P(), split, split)
    return jax.shard_map(body, mesh=fine, in_specs=placed, out_specs=P(), check_vma=False)
```

```python
import functools

import jax
import jax.numpy as jnp
from jax import lax
from jax.experimental import pallas as pl
from jax.experimental.pallas import tpu as pltpu
from jax.sharding import Mesh
from jax.sharding import PartitionSpec as P

HEAD_SIZE = 128
WINDOW_BLOCKS = 3
TOKENS = 256
RANK = 64
HEADS = 8
KEYS = (WINDOW_BLOCKS + 1) * TOKENS
FEATURES = HEADS * HEAD_SIZE + HEAD_SIZE
HALF = 640
CHUNK = 64
CHUNKS = [slice(i * CHUNK, (i + 1) * CHUNK) for i in range(KEYS // CHUNK)]
EARLY = 2
SHARE = 256
LINE = 2 * SHARE + 128
NEG_FILL = -1e30
SCALE = HEAD_SIZE ** (-0.5)
LOG2E = 1.4426950408889634

CTX = ("y", "z", "core")
VMEM = pl.BlockSpec(memory_space=pltpu.VMEM)
SMEM = pl.BlockSpec(memory_space=pltpu.SMEM)
NT = (((1,), (1,)), ((), ()))


def lanes(head):
    return slice(head * HEAD_SIZE, (head + 1) * HEAD_SIZE)


def folded(x):
    return x.reshape(x.shape[0] // 8, 8, TOKENS)


def visible_bias(place, stop):
    row = lax.broadcasted_iota(jnp.int32, (TOKENS, TOKENS), 0)
    col = lax.broadcasted_iota(jnp.int32, (TOKENS, TOKENS), 1)
    gap = col - row + stop * TOKENS
    key_pos = (place[0] - stop) * TOKENS + row
    allowed = (gap >= 0) & (gap < place[2]) & (key_pos < place[1]) & (key_pos >= 0)
    return jnp.where(allowed, 0.0, NEG_FILL)


def own_kernel(
    spot, lengths, stops, queries, cotangent, pack,
    weight_ref, dprob_ref, stat_ref, q_ref, g_ref, place, bias, score_buf,
):
    place[0] = spot[0]
    place[1] = lengths[spot[1]]
    place[2] = stops[spot[1]]
    token = lax.broadcasted_iota(jnp.int32, (TOKENS, HEAD_SIZE), 0)
    live = spot[0] * TOKENS + token < lengths[spot[1]]
    live = jnp.where(live, 1.0, 0.0).astype(jnp.bfloat16)
    for head in range(HEADS):
        q_ref[:, lanes(head)] = queries[:, lanes(head)]
        g_ref[:, lanes(head)] = cotangent[:, lanes(head)] * live
    block_kernel(0, place, q_ref, g_ref, pack, weight_ref, dprob_ref, stat_ref, bias, score_buf)


def block_kernel(
    stop, place, queries, cotangent, pack, weight_ref, dprob_ref, stat_ref, bias, score_buf
):
    bias[...] = visible_bias(place, stop)

    def products(head):
        score_buf[head % 2] = lax.dot_general(
            pack[0:TOKENS, :], queries[:, lanes(head)], NT, preferred_element_type=jnp.float32
        )
        dprob_ref[head] = lax.dot_general(
            pack[TOKENS : 2 * TOKENS, :],
            cotangent[:, lanes(head)],
            NT,
            preferred_element_type=jnp.float32,
        )

    products(0)
    for head in range(HEADS):
        if head + 1 < HEADS:
            products(head + 1)
        side = head % 2
        top = jnp.full((8, TOKENS), -3e38, jnp.float32)
        for rows in CHUNKS[: TOKENS // CHUNK]:
            scores = score_buf[side, rows] * (SCALE * LOG2E) + bias[rows]
            score_buf[side, rows] = scores
            top = jnp.maximum(top, jnp.max(folded(scores), axis=0))
        top = jnp.max(top, axis=0, keepdims=True)
        total = jnp.zeros((8, TOKENS), jnp.float32)
        inner = jnp.zeros((8, TOKENS), jnp.float32)
        for rows in CHUNKS[: TOKENS // CHUNK]:
            weights = jnp.exp2(score_buf[side, rows] - top)
            weight_ref[head, rows] = weights
            total = total + jnp.sum(folded(weights), axis=0)
            inner = inner + jnp.sum(folded(weights * dprob_ref[head, rows]), axis=0)
        stat_ref[head, 0:1, :] = top
        stat_ref[head, 1:2, :] = jnp.sum(total, axis=0, keepdims=True)
        stat_ref[head, 2:3, :] = jnp.sum(inner, axis=0, keepdims=True)


def attention_kernel(early_count, *refs):
    place, queries, cotangent, low_ref = refs[:4]
    packs = refs[4:8]
    early = [refs[8 + 3 * i : 11 + 3 * i] for i in range(early_count)]
    (
        keep_ref, send_ref, keys, values, keys_t, low_t, bias, sums,
        score_buf, dprob_buf, prob_buf, dscore_buf,
    ) = refs[8 + 3 * early_count :]
    core = place[0] % 2
    near = 1 + 2 * core
    stops = (0, 2, near, 4 - near)
    for slot in range(WINDOW_BLOCKS + 1):
        pack = packs[slot]
        rows = pl.ds(slot * TOKENS, TOKENS)
        key_block = pack[0:TOKENS, :]
        if slot >= early_count:
            fresh = pl.ds((slot - early_count) * TOKENS, TOKENS)
            keys[fresh, :] = key_block
            values[fresh, :] = pack[TOKENS : 2 * TOKENS, :]
            bias[fresh, :] = visible_bias(place, stops[slot])
        keys_t[:, rows] = key_block.T
        low_pair = pack[2 * TOKENS : 2 * TOKENS + 128, :].T
        low_t[:, slot * TOKENS : slot * TOKENS + 128] = low_pair[:RANK]
        low_t[:, slot * TOKENS + 128 : (slot + 1) * TOKENS] = low_pair[RANK:]
    query_low = low_ref[...].T[:RANK]
    offset = early_count * TOKENS
    fresh_chunks = CHUNKS[: (KEYS - offset) // CHUNK]

    def products(head):
        side = head % 2
        score_buf[side] = lax.dot_general(
            keys[...], queries[:, lanes(head)], NT, preferred_element_type=jnp.float32
        )
        dprob_buf[side] = lax.dot_general(
            values[...], cotangent[:, lanes(head)], NT, preferred_element_type=jnp.float32
        )

    def softmax(head):
        side = head % 2
        top = jnp.full((8, TOKENS), -3e38, jnp.float32)
        for rows in fresh_chunks:
            scores = score_buf[side, rows] * (SCALE * LOG2E) + bias[rows]
            score_buf[side, rows] = scores
            top = jnp.maximum(top, jnp.max(folded(scores), axis=0))
        top = jnp.max(top, axis=0, keepdims=True)
        for _, _, stat in early:
            top = jnp.maximum(top, stat[head, 0:1, :])
        total = jnp.zeros((8, TOKENS), jnp.float32)
        inner = jnp.zeros((8, TOKENS), jnp.float32)
        for rows in fresh_chunks:
            weights = jnp.exp2(score_buf[side, rows] - top)
            score_buf[side, rows] = weights
            total = total + jnp.sum(folded(weights), axis=0)
            inner = inner + jnp.sum(folded(weights * dprob_buf[side, rows]), axis=0)
        total = jnp.sum(total, axis=0, keepdims=True)
        inner = jnp.sum(inner, axis=0, keepdims=True)
        fades = []
        for _, _, stat in early:
            fade = jnp.exp2(stat[head, 0:1, :] - top)
            total = total + fade * stat[head, 1:2, :]
            inner = inner + fade * stat[head, 2:3, :]
            fades.append(fade)
        fraction = 1.0 / total
        inner = inner * fraction

        def settle(weights, dprob, factor, at):
            prob = weights * factor
            prob_buf[side, at : at + CHUNK] = prob.astype(jnp.bfloat16)
            dscore_buf[side, at : at + CHUNK] = (prob * (dprob - inner)).astype(jnp.bfloat16)

        for slot, (weight, dprob, _) in enumerate(early):
            factor = fades[slot] * fraction
            for rows in CHUNKS[: TOKENS // CHUNK]:
                settle(weight[head, rows], dprob[head, rows], factor, slot * TOKENS + rows.start)
        for rows in fresh_chunks:
            settle(score_buf[side, rows], dprob_buf[side, rows], fraction, offset + rows.start)

    def finish(head, value_sum):
        side = head % 2
        query_grad = jnp.dot(keys_t[...], dscore_buf[side], preferred_element_type=jnp.float32)
        query_grad = (query_grad * SCALE).astype(jnp.bfloat16)
        sums[head] = lax.dot_general(
            query_low, query_grad, NT, preferred_element_type=jnp.float32
        )
        g = cotangent[:, lanes(head)]
        return value_sum + jnp.dot(prob_buf[side], g, preferred_element_type=jnp.float32)

    value_sum = jnp.zeros((KEYS, HEAD_SIZE), jnp.float32)
    products(0)
    for head in range(HEADS):
        if head + 1 < HEADS:
            products(head + 1)
        if head > 0:
            value_sum = finish(head - 1, value_sum)
        softmax(head)
    value_sum = finish(HEADS - 1, value_sum)
    sums[HEADS] = jnp.dot(
        low_t[...], value_sum.astype(jnp.bfloat16), preferred_element_type=jnp.float32
    )
    for head in range(HEADS + 1):
        even = sums[head, pl.ds(0, 32, stride=2), :]
        odd = sums[head, pl.ds(1, 32, stride=2), :]
        keep_ref[:, lanes(head)] = jnp.where(core == 0, even, odd)
        send_ref[:, lanes(head)] = jnp.where(core == 0, odd, even)


def pair_kernel(keep_ref, got_ref, out_ref):
    total = keep_ref[...] + got_ref[...]
    upper = jnp.concatenate([total[:, HALF:], jnp.zeros((32, 2 * HALF - FEATURES))], axis=1)
    both = jnp.stack([total[:, :HALF], upper], axis=1).astype(jnp.bfloat16)
    out_ref[0:32] = both
    out_ref[32:64] = both


def score_kernel(rows_ref, up_query, up_value, out_ref):
    pieces = []
    squares = []
    for b in range(2):
        row = jnp.sum(rows_ref[b * 32 : (b + 1) * 32].astype(jnp.float32), axis=0)
        row = jnp.concatenate([row[0:1], row[1:2, : FEATURES - HALF]], axis=1)
        squares.append(jnp.sum(row * row))
        total = up_value[...] * row[:, HEADS * HEAD_SIZE :]
        for k in range(HEADS):
            total = total + up_query[pl.ds(k, SHARE, stride=HEADS), :] * row[
                :, k * HEAD_SIZE : (k + 1) * HEAD_SIZE
            ]
        pieces.append(jnp.sum(total.T, axis=0, keepdims=True))
    lane = lax.broadcasted_iota(jnp.int32, (1, 128), 1)
    tail = jnp.where(lane == 0, squares[0], jnp.where(lane == 1, squares[1], 0.0))
    line = jnp.concatenate(pieces + [tail], axis=1)
    for i in range(out_ref.shape[0]):
        out_ref[i] = line


def relay_kernel(in_ref, out_ref):
    line = jnp.sum(in_ref[...], axis=0)
    for i in range(out_ref.shape[0]):
        out_ref[i] = line


def final_kernel(in_ref, ids_ref, out_ref):
    halves = [jnp.sum(in_ref[s * 16 : (s + 1) * 16, :, :], axis=0) for s in range(2)]
    count = 2 * SHARE
    rest = []
    for b in range(2):
        square = halves[0][:, count + b : count + b + 1]
        part = [half[:, b * SHARE : (b + 1) * SHARE] for half in halves]
        scores = jnp.concatenate(part, axis=1) / jnp.sqrt(square + 1e-06)
        rest.append(scores)
    slot = lax.broadcasted_iota(jnp.int32, (count, count), 0)
    chosen = jnp.where(slot == ids_ref[...], 1.0, 0.0).astype(jnp.bfloat16)
    left = jnp.concatenate(rest, axis=0)
    pieces = []
    for _ in range(3):
        piece = left.astype(jnp.bfloat16)
        left = left - piece.astype(jnp.float32)
        pieces.append(piece.astype(jnp.float32))
    pieces.append(jnp.zeros((2, count), jnp.float32))
    stack = jnp.concatenate(pieces, axis=0).astype(jnp.bfloat16)
    total = jnp.dot(stack, chosen, preferred_element_type=jnp.float32)
    out_ref[...] = total[0:2] + total[2:4] + total[4:6]


def call(kernel, made, specs, scratch=(), flops=0, out_specs=None):
    return pl.pallas_call(
        kernel,
        out_shape=[jax.ShapeDtypeStruct(*one) for one in made],
        in_specs=specs,
        out_specs=out_specs or [VMEM] * len(made),
        scratch_shapes=list(scratch),
        compiler_params=pltpu.CompilerParams(vmem_limit_bytes=32 * 2**20),
        cost_estimate=pl.CostEstimate(flops=flops, bytes_accessed=2**20, transcendentals=0),
    )


def body(
    queries, attention_keys, attention_values, cotangent, low_rank, seq_lengths,
    window_stops, query_ids, query_up_gradients, value_up_gradients,
):
    low = low_rank[0]
    bf, f32 = jnp.bfloat16, jnp.float32
    halves = jnp.concatenate([low[:128, RANK:], low[128:, RANK:]], axis=1)
    pack = jnp.concatenate([attention_keys[0], attention_values[0], halves], axis=0)
    count = 64
    early = lax.ppermute(pack, CTX, [(i, i + 2) for i in range(count - 2)])
    apart = [(i, i + 1 + 2 * (i % 2)) for i in range(count) if i + 1 + 2 * (i % 2) < count]
    far = lax.ppermute(pack, CTX, apart)
    spot = jnp.stack([lax.axis_index(CTX), lax.axis_index("seq")]).astype(jnp.int32)
    tile = (TOKENS, TOKENS)
    scored = [((HEADS, *tile), f32), ((HEADS, *tile), f32), ((HEADS, 8, TOKENS), f32)]
    scratch = [pltpu.VMEM(tile, f32), pltpu.VMEM((2, *tile), f32)]
    flops = 2 * 2 * HEADS * TOKENS * TOKENS * HEAD_SIZE
    row = ((TOKENS, HEADS * HEAD_SIZE), bf)
    *own, q, g, place = call(
        own_kernel, scored + [row, row, ((3,), jnp.int32)],
        [SMEM] * 3 + [VMEM] * 3, scratch, flops, [VMEM] * 5 + [SMEM],
    )(spot, seq_lengths, window_stops, queries[0], cotangent[0], pack)
    early, own[2] = lax.optimization_barrier((early, own[2]))
    other = lax.ppermute(early, "core", [(0, 1), (1, 0)])
    near = call(
        functools.partial(block_kernel, 2), scored, [SMEM] + [VMEM] * 3, scratch, flops
    )(place, q, g, early)
    ready = [*own, *near]
    packs = [pack, early, other, far]
    fresh = KEYS - EARLY * TOKENS
    keep, send = call(
        functools.partial(attention_kernel, EARLY), [((RANK // 2, FEATURES), f32)] * 2,
        [SMEM] + [VMEM] * (7 + 3 * EARLY),
        [
            pltpu.VMEM((fresh, HEAD_SIZE), bf),
            pltpu.VMEM((fresh, HEAD_SIZE), bf),
            pltpu.VMEM((HEAD_SIZE, KEYS), bf),
            pltpu.VMEM((RANK, KEYS), bf),
            pltpu.VMEM((fresh, TOKENS), f32),
            pltpu.VMEM((HEADS + 1, RANK, HEAD_SIZE), f32),
            pltpu.VMEM((2, fresh, TOKENS), f32),
            pltpu.VMEM((2, fresh, TOKENS), f32),
            pltpu.VMEM((2, KEYS, TOKENS), bf),
            pltpu.VMEM((2, KEYS, TOKENS), bf),
        ],
        flops=2 * 4 * HEADS * TOKENS * KEYS * HEAD_SIZE,
    )(place, q, g, low, *packs, *ready)
    got = lax.ppermute(send, "core", [(0, 1), (1, 0)])
    (sums,) = call(pair_kernel, [((RANK, 2, HALF), bf)], [VMEM] * 2)(keep, got)
    sums = lax.all_to_all(sums, ("seq", "y", "z"), 0, 0, tiled=True)
    up_query = query_up_gradients.reshape(SHARE * HEADS, HEAD_SIZE)
    up_value = value_up_gradients.reshape(SHARE, HEAD_SIZE)
    (lines,) = call(score_kernel, [((16, 1, LINE), f32)], [VMEM] * 3)(sums, up_query, up_value)
    lines = lax.all_to_all(lines, ("z", "core"), 0, 0, tiled=True)
    (lines,) = call(relay_kernel, [((32, 1, LINE), f32)], [VMEM])(lines)
    lines = lax.all_to_all(lines, ("seq", "y", "tp"), 0, 0, tiled=True)
    (ranked,) = call(final_kernel, [((2, 2 * SHARE), f32)], [VMEM] * 2)(
        lines, query_ids.reshape(1, 2 * SHARE)
    )
    return ranked.T


def solution(mesh):
    fine = Mesh(mesh.devices.reshape(4, 8, 2, 4, 2), ("y", "z", "core", "tp", "seq"))
    split = P("seq", CTX, "tp")
    placed = (split, split, split, split, P("seq", CTX, None), P(), P(), P(), split, split)
    return jax.shard_map(body, mesh=fine, in_specs=placed, out_specs=P(), check_vma=False)
```

```python
import functools

import jax
import jax.numpy as jnp
from jax import lax
from jax.experimental import pallas as pl
from jax.experimental.pallas import tpu as pltpu
from jax.sharding import Mesh
from jax.sharding import PartitionSpec as P

HEAD_SIZE = 128
WINDOW_BLOCKS = 3
TOKENS = 256
RANK = 64
HEADS = 8
KEYS = (WINDOW_BLOCKS + 1) * TOKENS
FEATURES = HEADS * HEAD_SIZE + HEAD_SIZE
HALF = 640
PACK = 2 * TOKENS + 128
CHUNK = 64
CHUNKS = [slice(i * CHUNK, (i + 1) * CHUNK) for i in range(KEYS // CHUNK)]
EARLY = 2
SHARE = 256
LINE = 2 * SHARE + 128
NEG_FILL = -1e30
SCALE = HEAD_SIZE ** (-0.5)
LOG2E = 1.4426950408889634

CTX = ("y", "z", "core")
VMEM = pl.BlockSpec(memory_space=pltpu.VMEM)
SMEM = pl.BlockSpec(memory_space=pltpu.SMEM)
NT = (((1,), (1,)), ((), ()))


def lanes(head):
    return slice(head * HEAD_SIZE, (head + 1) * HEAD_SIZE)


def folded(x):
    return x.reshape(x.shape[0] // 8, 8, TOKENS)


def visible_bias(place, stop):
    row = lax.broadcasted_iota(jnp.int32, (TOKENS, TOKENS), 0)
    col = lax.broadcasted_iota(jnp.int32, (TOKENS, TOKENS), 1)
    gap = col - row + stop * TOKENS
    key_pos = (place[0] - stop) * TOKENS + row
    allowed = (gap >= 0) & (gap < place[2]) & (key_pos < place[1]) & (key_pos >= 0)
    return jnp.where(allowed, 0.0, NEG_FILL)


def pack_kernel(in_ref, out_ref):
    out_ref[0 : 2 * TOKENS, :] = in_ref[0 : 2 * TOKENS, :]
    low = in_ref[2 * TOKENS : 3 * TOKENS, RANK:].astype(jnp.float32)
    low = jnp.concatenate([low[:128], low[128:]], axis=1)
    out_ref[2 * TOKENS :, :] = low.astype(jnp.bfloat16)


def own_kernel(
    spot, both, pack, weight_ref, dprob_ref, stat_ref, g_ref, place, bias, score_buf
):
    place[0] = spot[0]
    place[1] = spot[2 + spot[1]]
    place[2] = spot[4 + spot[1]]
    token = lax.broadcasted_iota(jnp.int32, (TOKENS, HEAD_SIZE), 0)
    live = spot[0] * TOKENS + token < spot[2 + spot[1]]
    live = jnp.where(live, 1.0, 0.0).astype(jnp.bfloat16)
    for head in range(HEADS):
        g_ref[:, lanes(head)] = both[TOKENS : 2 * TOKENS, lanes(head)] * live
    block_kernel(0, place, both, g_ref, pack, weight_ref, dprob_ref, stat_ref, bias, score_buf)


def block_kernel(
    stop, place, queries, cotangent, pack, weight_ref, dprob_ref, stat_ref, bias, score_buf
):
    bias[...] = visible_bias(place, stop)

    def products(head):
        score_buf[head % 2] = lax.dot_general(
            pack[0:TOKENS, :], queries[0:TOKENS, lanes(head)], NT, preferred_element_type=jnp.float32
        )
        dprob_ref[head] = lax.dot_general(
            pack[TOKENS : 2 * TOKENS, :],
            cotangent[:, lanes(head)],
            NT,
            preferred_element_type=jnp.float32,
        )

    products(0)
    for head in range(HEADS):
        if head + 1 < HEADS:
            products(head + 1)
        side = head % 2
        top = jnp.full((8, TOKENS), -3e38, jnp.float32)
        for rows in CHUNKS[: TOKENS // CHUNK]:
            scores = score_buf[side, rows] * (SCALE * LOG2E) + bias[rows]
            score_buf[side, rows] = scores
            top = jnp.maximum(top, jnp.max(folded(scores), axis=0))
        top = jnp.max(top, axis=0, keepdims=True)
        total = jnp.zeros((8, TOKENS), jnp.float32)
        inner = jnp.zeros((8, TOKENS), jnp.float32)
        for rows in CHUNKS[: TOKENS // CHUNK]:
            weights = jnp.exp2(score_buf[side, rows] - top)
            weight_ref[head, rows] = weights
            total = total + jnp.sum(folded(weights), axis=0)
            inner = inner + jnp.sum(folded(weights * dprob_ref[head, rows]), axis=0)
        stat_ref[head, 0:1, :] = top
        stat_ref[head, 1:2, :] = jnp.sum(total, axis=0, keepdims=True)
        stat_ref[head, 2:3, :] = jnp.sum(inner, axis=0, keepdims=True)


def attention_kernel(early_count, *refs):
    place, queries, cotangent, low_ref = refs[:4]
    packs = refs[4:8]
    early = [refs[8 + 3 * i : 11 + 3 * i] for i in range(early_count)]
    (
        keep_ref, send_ref, keys, values, keys_t, low_t, bias, sums,
        score_buf, dprob_buf, prob_buf, dscore_buf,
    ) = refs[8 + 3 * early_count :]
    core = place[0] % 2
    near = 1 + 2 * core
    stops = (0, 2, near, 4 - near)
    for slot in range(WINDOW_BLOCKS + 1):
        pack = packs[slot]
        base = pl.multiple_of((1 - core) * PACK, PACK) if slot == 2 else 0
        rows = pl.ds(slot * TOKENS, TOKENS)
        key_block = pack[pl.ds(base, TOKENS), :]
        if slot >= early_count:
            fresh = pl.ds((slot - early_count) * TOKENS, TOKENS)
            keys[fresh, :] = key_block
            values[fresh, :] = pack[pl.ds(base + TOKENS, TOKENS), :]
            bias[fresh, :] = visible_bias(place, stops[slot])
        keys_t[:, rows] = key_block.T
        low_pair = pack[pl.ds(base + 2 * TOKENS, 128), :].T
        low_t[:, slot * TOKENS : slot * TOKENS + 128] = low_pair[:RANK]
        low_t[:, slot * TOKENS + 128 : (slot + 1) * TOKENS] = low_pair[RANK:]
    query_low = low_ref[2 * TOKENS : 3 * TOKENS, :].T[:RANK]
    offset = early_count * TOKENS
    fresh_chunks = CHUNKS[: (KEYS - offset) // CHUNK]

    def products(head):
        side = head % 2
        score_buf[side] = lax.dot_general(
            keys[...], queries[0:TOKENS, lanes(head)], NT, preferred_element_type=jnp.float32
        )
        dprob_buf[side] = lax.dot_general(
            values[...], cotangent[:, lanes(head)], NT, preferred_element_type=jnp.float32
        )

    def softmax(head):
        side = head % 2
        top = jnp.full((8, TOKENS), -3e38, jnp.float32)
        for rows in fresh_chunks:
            scores = score_buf[side, rows] * (SCALE * LOG2E) + bias[rows]
            score_buf[side, rows] = scores
            top = jnp.maximum(top, jnp.max(folded(scores), axis=0))
        top = jnp.max(top, axis=0, keepdims=True)
        for _, _, stat in early:
            top = jnp.maximum(top, stat[head, 0:1, :])
        total = jnp.zeros((8, TOKENS), jnp.float32)
        inner = jnp.zeros((8, TOKENS), jnp.float32)
        for rows in fresh_chunks:
            weights = jnp.exp2(score_buf[side, rows] - top)
            score_buf[side, rows] = weights
            total = total + jnp.sum(folded(weights), axis=0)
            inner = inner + jnp.sum(folded(weights * dprob_buf[side, rows]), axis=0)
        total = jnp.sum(total, axis=0, keepdims=True)
        inner = jnp.sum(inner, axis=0, keepdims=True)
        fades = []
        for _, _, stat in early:
            fade = jnp.exp2(stat[head, 0:1, :] - top)
            total = total + fade * stat[head, 1:2, :]
            inner = inner + fade * stat[head, 2:3, :]
            fades.append(fade)
        fraction = 1.0 / total
        inner = inner * fraction

        def settle(weights, dprob, factor, at):
            prob = weights * factor
            prob_buf[side, at : at + CHUNK] = prob.astype(jnp.bfloat16)
            dscore_buf[side, at : at + CHUNK] = (prob * (dprob - inner)).astype(jnp.bfloat16)

        for slot, (weight, dprob, _) in enumerate(early):
            factor = fades[slot] * fraction
            for rows in CHUNKS[: TOKENS // CHUNK]:
                settle(weight[head, rows], dprob[head, rows], factor, slot * TOKENS + rows.start)
        for rows in fresh_chunks:
            settle(score_buf[side, rows], dprob_buf[side, rows], fraction, offset + rows.start)

    def finish(head, value_sum):
        side = head % 2
        query_grad = jnp.dot(keys_t[...], dscore_buf[side], preferred_element_type=jnp.float32)
        query_grad = (query_grad * SCALE).astype(jnp.bfloat16)
        sums[head] = lax.dot_general(
            query_low, query_grad, NT, preferred_element_type=jnp.float32
        )
        g = cotangent[:, lanes(head)]
        return value_sum + jnp.dot(prob_buf[side], g, preferred_element_type=jnp.float32)

    value_sum = jnp.zeros((KEYS, HEAD_SIZE), jnp.float32)
    products(0)
    for head in range(HEADS):
        if head + 1 < HEADS:
            products(head + 1)
        if head > 0:
            value_sum = finish(head - 1, value_sum)
        softmax(head)
    value_sum = finish(HEADS - 1, value_sum)
    sums[HEADS] = jnp.dot(
        low_t[...], value_sum.astype(jnp.bfloat16), preferred_element_type=jnp.float32
    )
    for head in range(HEADS + 1):
        even = sums[head, pl.ds(0, 32, stride=2), :]
        odd = sums[head, pl.ds(1, 32, stride=2), :]
        keep_ref[:, lanes(head)] = jnp.where(core == 0, even, odd)
        send_ref[:, lanes(head)] = jnp.where(core == 0, odd, even)


def pair_kernel(place, keep_ref, got_ref, out_ref):
    rows = RANK // 2
    start = pl.multiple_of((1 - place[0] % 2) * rows, rows)
    total = keep_ref[...] + got_ref[pl.ds(start, rows), :]
    upper = jnp.concatenate([total[:, HALF:], jnp.zeros((32, 2 * HALF - FEATURES))], axis=1)
    both = jnp.stack([total[:, :HALF], upper], axis=1).astype(jnp.bfloat16)
    for y in range(out_ref.shape[1]):
        for seq in range(2):
            out_ref[:, y, seq] = both[y * 8 : (y + 1) * 8]


def score_kernel(rows_ref, up_query, up_value, out_ref):
    pieces = []
    squares = []
    for b in range(2):
        row = jnp.sum(rows_ref[:, b].astype(jnp.float32), axis=0)
        row = jnp.concatenate([row[0:1], row[1:2, : FEATURES - HALF]], axis=1)
        squares.append(jnp.sum(row * row))
        total = up_value[...] * row[:, HEADS * HEAD_SIZE :]
        for k in range(HEADS):
            total = total + up_query[pl.ds(k, SHARE, stride=HEADS), :] * row[
                :, k * HEAD_SIZE : (k + 1) * HEAD_SIZE
            ]
        pieces.append(jnp.sum(total.T, axis=0, keepdims=True))
    lane = lax.broadcasted_iota(jnp.int32, (1, 128), 1)
    tail = jnp.where(lane == 0, squares[0], jnp.where(lane == 1, squares[1], 0.0))
    line = jnp.concatenate(pieces + [tail], axis=1)
    for i in range(out_ref.shape[0]):
        out_ref[i] = line


def relay_kernel(in_ref, out_ref):
    line = jnp.sum(in_ref[...], axis=0)
    for i in range(out_ref.shape[0]):
        out_ref[i] = line


def final_kernel(in_ref, ids_ref, out_ref):
    halves = [jnp.sum(in_ref[:, s], axis=0) for s in range(2)]
    count = 2 * SHARE
    rest = []
    for b in range(2):
        square = halves[0][:, count + b : count + b + 1]
        part = [half[:, b * SHARE : (b + 1) * SHARE] for half in halves]
        scores = jnp.concatenate(part, axis=1) / jnp.sqrt(square + 1e-06)
        rest.append(scores)
    slot = lax.broadcasted_iota(jnp.int32, (count, count), 0)
    chosen = jnp.where(slot == ids_ref[...], 1.0, 0.0).astype(jnp.bfloat16)
    left = jnp.concatenate(rest, axis=0)
    pieces = []
    for _ in range(3):
        piece = left.astype(jnp.bfloat16)
        left = left - piece.astype(jnp.float32)
        pieces.append(piece.astype(jnp.float32))
    pieces.append(jnp.zeros((2, count), jnp.float32))
    stack = jnp.concatenate(pieces, axis=0).astype(jnp.bfloat16)
    total = jnp.dot(stack, chosen, preferred_element_type=jnp.float32)
    out_ref[...] = total[0:2] + total[2:4] + total[4:6]


def call(kernel, made, specs, scratch=(), flops=0, out_specs=None):
    return pl.pallas_call(
        kernel,
        out_shape=[jax.ShapeDtypeStruct(*one) for one in made],
        in_specs=specs,
        out_specs=out_specs or [VMEM] * len(made),
        scratch_shapes=list(scratch),
        compiler_params=pltpu.CompilerParams(vmem_limit_bytes=32 * 2**20),
        cost_estimate=pl.CostEstimate(flops=flops, bytes_accessed=2**20, transcendentals=0),
    )


def body(
    queries, attention_keys, attention_values, cotangent, low_rank, seq_lengths,
    window_stops, query_ids, query_up_gradients, value_up_gradients,
):
    bf, f32 = jnp.bfloat16, jnp.float32
    three = jnp.concatenate([attention_keys[0], attention_values[0], low_rank[0]], axis=0)
    (pack,) = call(pack_kernel, [((PACK, HEAD_SIZE), bf)], [VMEM])(three)
    count = 64
    early = lax.ppermute(pack, CTX, [(i, i + 2) for i in range(count - 2)])
    apart = [(i, i + 1 + 2 * (i % 2)) for i in range(count) if i + 1 + 2 * (i % 2) < count]
    spot = jnp.stack([lax.axis_index(CTX), lax.axis_index("seq")]).astype(jnp.int32)
    spot = jnp.concatenate([spot, seq_lengths, window_stops])
    both = jnp.concatenate([queries[0], cotangent[0]], axis=0)
    later, both = lax.optimization_barrier((pack, both))
    far = lax.ppermute(later, CTX, apart)
    tile = (TOKENS, TOKENS)
    scored = [((HEADS, *tile), f32), ((HEADS, *tile), f32), ((HEADS, 8, TOKENS), f32)]
    scratch = [pltpu.VMEM(tile, f32), pltpu.VMEM((2, *tile), f32)]
    flops = 2 * 2 * HEADS * TOKENS * TOKENS * HEAD_SIZE
    row = ((TOKENS, HEADS * HEAD_SIZE), bf)
    *own, g, place = call(
        own_kernel, scored + [row, ((3,), jnp.int32)],
        [SMEM] + [VMEM] * 2, scratch, flops, [VMEM] * 4 + [SMEM],
    )(spot, both, pack)
    early, own[2] = lax.optimization_barrier((early, own[2]))
    other = lax.all_gather(early, "core", axis=0, tiled=True)
    near = call(
        functools.partial(block_kernel, 2), scored, [SMEM] + [VMEM] * 3, scratch, flops
    )(place, both, g, early)
    ready = [*own, *near]
    packs = [pack, early, other, far]
    fresh = KEYS - EARLY * TOKENS
    keep, send = call(
        functools.partial(attention_kernel, EARLY), [((RANK // 2, FEATURES), f32)] * 2,
        [SMEM] + [VMEM] * (7 + 3 * EARLY),
        [
            pltpu.VMEM((fresh, HEAD_SIZE), bf),
            pltpu.VMEM((fresh, HEAD_SIZE), bf),
            pltpu.VMEM((HEAD_SIZE, KEYS), bf),
            pltpu.VMEM((RANK, KEYS), bf),
            pltpu.VMEM((fresh, TOKENS), f32),
            pltpu.VMEM((HEADS + 1, RANK, HEAD_SIZE), f32),
            pltpu.VMEM((2, fresh, TOKENS), f32),
            pltpu.VMEM((2, fresh, TOKENS), f32),
            pltpu.VMEM((2, KEYS, TOKENS), bf),
            pltpu.VMEM((2, KEYS, TOKENS), bf),
        ],
        flops=2 * 4 * HEADS * TOKENS * KEYS * HEAD_SIZE,
    )(place, both, g, three, *packs, *ready)
    got = lax.all_gather(send, "core", axis=0, tiled=True)
    (sums,) = call(pair_kernel, [((8, 4, 2, 2, HALF), bf)], [SMEM] + [VMEM] * 2)(
        place, keep, got
    )
    sums = lax.all_to_all(sums.reshape(RANK, 2, HALF), ("z", "y", "seq"), 0, 0, tiled=True)
    up_query = query_up_gradients.reshape(SHARE * HEADS, HEAD_SIZE)
    up_value = value_up_gradients.reshape(SHARE, HEAD_SIZE)
    (lines,) = call(score_kernel, [((16, 1, LINE), f32)], [VMEM] * 3)(
        sums.reshape(RANK // 2, 2, 2, HALF), up_query, up_value
    )
    lines = lax.all_to_all(lines, ("z", "core"), 0, 0, tiled=True)
    (lines,) = call(relay_kernel, [((32, 1, LINE), f32)], [VMEM])(lines)
    lines = lax.all_to_all(lines, ("tp", "y", "seq"), 0, 0, tiled=True)
    (ranked,) = call(final_kernel, [((2, 2 * SHARE), f32)], [VMEM] * 2)(
        lines.reshape(16, 2, 1, LINE), query_ids.reshape(1, 2 * SHARE)
    )
    return ranked.T


def solution(mesh):
    fine = Mesh(mesh.devices.reshape(4, 8, 2, 4, 2), ("y", "z", "core", "tp", "seq"))
    split = P("seq", CTX, "tp")
    placed = (split, split, split, split, P("seq", CTX, None), P(), P(), P(), split, split)
    return jax.shard_map(body, mesh=fine, in_specs=placed, out_specs=P(), check_vma=False)
```

```python
import functools

import jax
import jax.numpy as jnp
from jax import lax
from jax.experimental import pallas as pl
from jax.experimental.pallas import tpu as pltpu
from jax.sharding import Mesh
from jax.sharding import PartitionSpec as P

HEAD_SIZE = 128
WINDOW_BLOCKS = 3
TOKENS = 256
RANK = 64
HEADS = 8
KEYS = (WINDOW_BLOCKS + 1) * TOKENS
FEATURES = HEADS * HEAD_SIZE + HEAD_SIZE
HALF = 640
PACK = 2 * TOKENS + 128
CHUNK = 64
CHUNKS = [slice(i * CHUNK, (i + 1) * CHUNK) for i in range(KEYS // CHUNK)]
EARLY = 2
SHARE = 256
LINE = 2 * SHARE + 128
NEG_FILL = -1e30
SCALE = HEAD_SIZE ** (-0.5)
LOG2E = 1.4426950408889634

CTX = ("y", "z", "core")
VMEM = pl.BlockSpec(memory_space=pltpu.VMEM)
SMEM = pl.BlockSpec(memory_space=pltpu.SMEM)
NT = (((1,), (1,)), ((), ()))


def lanes(head):
    return slice(head * HEAD_SIZE, (head + 1) * HEAD_SIZE)


def folded(x):
    return x.reshape(x.shape[0] // 8, 8, TOKENS)


def visible_bias(place, stop):
    row = lax.broadcasted_iota(jnp.int32, (TOKENS, TOKENS), 0)
    col = lax.broadcasted_iota(jnp.int32, (TOKENS, TOKENS), 1)
    gap = col - row + stop * TOKENS
    key_pos = (place[0] - stop) * TOKENS + row
    allowed = (gap >= 0) & (gap < place[2]) & (key_pos < place[1]) & (key_pos >= 0)
    return jnp.where(allowed, 0.0, NEG_FILL)


def pack_kernel(in_ref, out_ref):
    out_ref[0 : 2 * TOKENS, :] = in_ref[0 : 2 * TOKENS, :]
    low = in_ref[2 * TOKENS : 3 * TOKENS, RANK:].astype(jnp.float32)
    low = jnp.concatenate([low[:128], low[128:]], axis=1)
    out_ref[2 * TOKENS :, :] = low.astype(jnp.bfloat16)


def own_kernel(
    spot, both, pack, weight_ref, dprob_ref, stat_ref, g_ref, place, bias, score_buf
):
    place[0] = spot[0]
    place[1] = spot[2 + spot[1]]
    place[2] = spot[4 + spot[1]]
    token = lax.broadcasted_iota(jnp.int32, (TOKENS, HEAD_SIZE), 0)
    live = spot[0] * TOKENS + token < spot[2 + spot[1]]
    live = jnp.where(live, 1.0, 0.0).astype(jnp.bfloat16)
    for head in range(HEADS):
        g_ref[:, lanes(head)] = both[TOKENS : 2 * TOKENS, lanes(head)] * live
    block_kernel(0, place, both, g_ref, pack, weight_ref, dprob_ref, stat_ref, bias, score_buf)


def block_kernel(
    stop, place, queries, cotangent, pack, weight_ref, dprob_ref, stat_ref, bias, score_buf
):
    bias[...] = visible_bias(place, stop)

    def products(head):
        score_buf[head % 2] = lax.dot_general(
            pack[0:TOKENS, :], queries[0:TOKENS, lanes(head)], NT, preferred_element_type=jnp.float32
        )
        dprob_ref[head] = lax.dot_general(
            pack[TOKENS : 2 * TOKENS, :],
            cotangent[:, lanes(head)],
            NT,
            preferred_element_type=jnp.float32,
        )

    products(0)
    for head in range(HEADS):
        if head + 1 < HEADS:
            products(head + 1)
        side = head % 2
        top = jnp.full((8, TOKENS), -3e38, jnp.float32)
        for rows in CHUNKS[: TOKENS // CHUNK]:
            scores = score_buf[side, rows] * (SCALE * LOG2E) + bias[rows]
            score_buf[side, rows] = scores
            top = jnp.maximum(top, jnp.max(folded(scores), axis=0))
        top = jnp.max(top, axis=0, keepdims=True)
        total = jnp.zeros((8, TOKENS), jnp.float32)
        inner = jnp.zeros((8, TOKENS), jnp.float32)
        for rows in CHUNKS[: TOKENS // CHUNK]:
            weights = jnp.exp2(score_buf[side, rows] - top)
            weight_ref[head, rows] = weights
            total = total + jnp.sum(folded(weights), axis=0)
            inner = inner + jnp.sum(folded(weights * dprob_ref[head, rows]), axis=0)
        stat_ref[head, 0:1, :] = top
        stat_ref[head, 1:2, :] = jnp.sum(total, axis=0, keepdims=True)
        stat_ref[head, 2:3, :] = jnp.sum(inner, axis=0, keepdims=True)


def attention_kernel(early_count, *refs):
    place, queries, cotangent, low_ref = refs[:4]
    packs = refs[4:8]
    early = [refs[8 + 3 * i : 11 + 3 * i] for i in range(early_count)]
    (
        keep_ref, send_ref, keys, values, keys_t, low_t, bias, sums,
        score_buf, dprob_buf, prob_buf, dscore_buf,
    ) = refs[8 + 3 * early_count :]
    core = place[0] % 2
    near = 1 + 2 * core
    stops = (0, 2, near, 4 - near)
    for slot in range(WINDOW_BLOCKS + 1):
        pack = packs[slot]
        rows = pl.ds(slot * TOKENS, TOKENS)
        key_block = pack[0:TOKENS, :]
        if slot >= early_count:
            fresh = pl.ds((slot - early_count) * TOKENS, TOKENS)
            keys[fresh, :] = key_block
            values[fresh, :] = pack[TOKENS : 2 * TOKENS, :]
            bias[fresh, :] = visible_bias(place, stops[slot])
        keys_t[:, rows] = key_block.T
        low_pair = pack[2 * TOKENS : PACK, :].T
        low_t[:, slot * TOKENS : slot * TOKENS + 128] = low_pair[:RANK]
        low_t[:, slot * TOKENS + 128 : (slot + 1) * TOKENS] = low_pair[RANK:]
    to = lax.broadcasted_iota(jnp.int32, (RANK, RANK), 0)
    source = lax.broadcasted_iota(jnp.int32, (RANK, RANK), 1)
    order = (to % 4) * 16 + (to % 32) // 4 * 2 + to // 32
    order = jnp.where(source == order, 1.0, 0.0).astype(jnp.bfloat16)
    query_low = low_ref[2 * TOKENS : 3 * TOKENS, :].T[:RANK]
    query_low = jnp.dot(order, query_low, preferred_element_type=jnp.float32).astype(jnp.bfloat16)
    value_low = jnp.dot(order, low_t[...], preferred_element_type=jnp.float32).astype(jnp.bfloat16)
    offset = early_count * TOKENS
    fresh_chunks = CHUNKS[: (KEYS - offset) // CHUNK]

    def products(head):
        side = head % 2
        score_buf[side] = lax.dot_general(
            keys[...], queries[0:TOKENS, lanes(head)], NT, preferred_element_type=jnp.float32
        )
        dprob_buf[side] = lax.dot_general(
            values[...], cotangent[:, lanes(head)], NT, preferred_element_type=jnp.float32
        )

    def softmax(head):
        side = head % 2
        top = jnp.full((8, TOKENS), -3e38, jnp.float32)
        for rows in fresh_chunks:
            scores = score_buf[side, rows] * (SCALE * LOG2E) + bias[rows]
            score_buf[side, rows] = scores
            top = jnp.maximum(top, jnp.max(folded(scores), axis=0))
        top = jnp.max(top, axis=0, keepdims=True)
        for _, _, stat in early:
            top = jnp.maximum(top, stat[head, 0:1, :])
        total = jnp.zeros((8, TOKENS), jnp.float32)
        inner = jnp.zeros((8, TOKENS), jnp.float32)
        for rows in fresh_chunks:
            weights = jnp.exp2(score_buf[side, rows] - top)
            score_buf[side, rows] = weights
            total = total + jnp.sum(folded(weights), axis=0)
            inner = inner + jnp.sum(folded(weights * dprob_buf[side, rows]), axis=0)
        total = jnp.sum(total, axis=0, keepdims=True)
        inner = jnp.sum(inner, axis=0, keepdims=True)
        fades = []
        for _, _, stat in early:
            fade = jnp.exp2(stat[head, 0:1, :] - top)
            total = total + fade * stat[head, 1:2, :]
            inner = inner + fade * stat[head, 2:3, :]
            fades.append(fade)
        fraction = 1.0 / total
        inner = inner * fraction

        def settle(weights, dprob, factor, at):
            prob = weights * factor
            prob_buf[side, at : at + CHUNK] = prob.astype(jnp.bfloat16)
            dscore_buf[side, at : at + CHUNK] = (prob * (dprob - inner)).astype(jnp.bfloat16)

        for slot, (weight, dprob, _) in enumerate(early):
            factor = fades[slot] * fraction
            for rows in CHUNKS[: TOKENS // CHUNK]:
                settle(weight[head, rows], dprob[head, rows], factor, slot * TOKENS + rows.start)
        for rows in fresh_chunks:
            settle(score_buf[side, rows], dprob_buf[side, rows], fraction, offset + rows.start)

    def finish(head, value_sum):
        side = head % 2
        query_grad = jnp.dot(keys_t[...], dscore_buf[side], preferred_element_type=jnp.float32)
        query_grad = (query_grad * SCALE).astype(jnp.bfloat16)
        sums[head] = lax.dot_general(
            query_low, query_grad, NT, preferred_element_type=jnp.float32
        )
        g = cotangent[:, lanes(head)]
        return value_sum + jnp.dot(prob_buf[side], g, preferred_element_type=jnp.float32)

    value_sum = jnp.zeros((KEYS, HEAD_SIZE), jnp.float32)
    products(0)
    for head in range(HEADS):
        if head + 1 < HEADS:
            products(head + 1)
        if head > 0:
            value_sum = finish(head - 1, value_sum)
        softmax(head)
    value_sum = finish(HEADS - 1, value_sum)
    sums[HEADS] = jnp.dot(
        value_low, value_sum.astype(jnp.bfloat16), preferred_element_type=jnp.float32
    )
    for head in range(HEADS + 1):
        even = sums[head, 0:32, :]
        odd = sums[head, 32:64, :]
        keep_ref[:, lanes(head)] = jnp.where(core == 0, even, odd)
        send_ref[:, lanes(head)] = jnp.where(core == 0, odd, even)


def pair_kernel(place, keep_ref, got_ref, out_ref):
    rows = RANK // 2
    start = pl.multiple_of((1 - place[0] % 2) * rows, rows)
    total = keep_ref[...] + got_ref[pl.ds(start, rows), :]
    upper = jnp.concatenate([total[:, HALF:], jnp.zeros((32, 2 * HALF - FEATURES))], axis=1)
    both = jnp.stack([total[:, :HALF], upper], axis=1).astype(jnp.bfloat16)
    for seq in range(2):
        out_ref[:, seq] = both


def score_kernel(rows_ref, up_query, up_value, out_ref):
    pieces = []
    squares = []
    for b in range(2):
        row = jnp.sum(rows_ref[:, b].astype(jnp.float32), axis=0)
        row = jnp.concatenate([row[0:1], row[1:2, : FEATURES - HALF]], axis=1)
        squares.append(jnp.sum(row * row))
        total = up_value[...] * row[:, HEADS * HEAD_SIZE :]
        for k in range(HEADS):
            total = total + up_query[pl.ds(k, SHARE, stride=HEADS), :] * row[
                :, k * HEAD_SIZE : (k + 1) * HEAD_SIZE
            ]
        pieces.append(jnp.sum(total.T, axis=0, keepdims=True))
    lane = lax.broadcasted_iota(jnp.int32, (1, 128), 1)
    tail = jnp.where(lane == 0, squares[0], jnp.where(lane == 1, squares[1], 0.0))
    line = jnp.concatenate(pieces + [tail], axis=1)
    for i in range(out_ref.shape[0]):
        out_ref[i] = line


def relay_kernel(in_ref, out_ref):
    line = jnp.sum(in_ref[...], axis=0)
    for i in range(out_ref.shape[0]):
        out_ref[i] = line


def final_kernel(in_ref, ids_ref, out_ref):
    halves = [jnp.sum(in_ref[:, s], axis=0) for s in range(2)]
    count = 2 * SHARE
    rest = []
    for b in range(2):
        square = halves[0][:, count + b : count + b + 1]
        part = [half[:, b * SHARE : (b + 1) * SHARE] for half in halves]
        scores = jnp.concatenate(part, axis=1) / jnp.sqrt(square + 1e-06)
        rest.append(scores)
    slot = lax.broadcasted_iota(jnp.int32, (count, count), 0)
    chosen = jnp.where(slot == ids_ref[...], 1.0, 0.0).astype(jnp.bfloat16)
    left = jnp.concatenate(rest, axis=0)
    pieces = []
    for _ in range(3):
        piece = left.astype(jnp.bfloat16)
        left = left - piece.astype(jnp.float32)
        pieces.append(piece.astype(jnp.float32))
    pieces.append(jnp.zeros((2, count), jnp.float32))
    stack = jnp.concatenate(pieces, axis=0).astype(jnp.bfloat16)
    total = jnp.dot(stack, chosen, preferred_element_type=jnp.float32)
    out_ref[...] = total[0:2] + total[2:4] + total[4:6]


def call(kernel, made, specs, scratch=(), flops=0, out_specs=None):
    return pl.pallas_call(
        kernel,
        out_shape=[jax.ShapeDtypeStruct(*one) for one in made],
        in_specs=specs,
        out_specs=out_specs or [VMEM] * len(made),
        scratch_shapes=list(scratch),
        compiler_params=pltpu.CompilerParams(vmem_limit_bytes=32 * 2**20),
        cost_estimate=pl.CostEstimate(flops=flops, bytes_accessed=2**20, transcendentals=0),
    )


def body(
    queries, attention_keys, attention_values, cotangent, low_rank, seq_lengths,
    window_stops, query_ids, query_up_gradients, value_up_gradients,
):
    bf, f32 = jnp.bfloat16, jnp.float32
    three = jnp.concatenate([attention_keys[0], attention_values[0], low_rank[0]], axis=0)
    (pack,) = call(pack_kernel, [((PACK, HEAD_SIZE), bf)], [VMEM])(three)
    count = 64
    early = lax.ppermute(pack, CTX, [(i, i + 2) for i in range(count - 2)])
    apart = [(i, i + 1 + 2 * (i % 2)) for i in range(count) if i + 1 + 2 * (i % 2) < count]
    spot = jnp.stack([lax.axis_index(CTX), lax.axis_index("seq")]).astype(jnp.int32)
    spot = jnp.concatenate([spot, seq_lengths, window_stops])
    both = jnp.concatenate([queries[0], cotangent[0]], axis=0)
    later, both = lax.optimization_barrier((pack, both))
    far = lax.ppermute(later, CTX, apart)
    tile = (TOKENS, TOKENS)
    scored = [((HEADS, *tile), f32), ((HEADS, *tile), f32), ((HEADS, 8, TOKENS), f32)]
    scratch = [pltpu.VMEM(tile, f32), pltpu.VMEM((2, *tile), f32)]
    flops = 2 * 2 * HEADS * TOKENS * TOKENS * HEAD_SIZE
    row = ((TOKENS, HEADS * HEAD_SIZE), bf)
    *own, g, place = call(
        own_kernel, scored + [row, ((3,), jnp.int32)],
        [SMEM] + [VMEM] * 2, scratch, flops, [VMEM] * 4 + [SMEM],
    )(spot, both, pack)
    early, own[2] = lax.optimization_barrier((early, own[2]))
    other = lax.ppermute(early, "core", [(0, 1), (1, 0)])
    near = call(
        functools.partial(block_kernel, 2), scored, [SMEM] + [VMEM] * 3, scratch, flops
    )(place, both, g, early)
    ready = [*own, *near]
    packs = [pack, early, other, far]
    fresh = KEYS - EARLY * TOKENS
    keep, send = call(
        functools.partial(attention_kernel, EARLY), [((RANK // 2, FEATURES), f32)] * 2,
        [SMEM] + [VMEM] * (7 + 3 * EARLY),
        [
            pltpu.VMEM((fresh, HEAD_SIZE), bf),
            pltpu.VMEM((fresh, HEAD_SIZE), bf),
            pltpu.VMEM((HEAD_SIZE, KEYS), bf),
            pltpu.VMEM((RANK, KEYS), bf),
            pltpu.VMEM((fresh, TOKENS), f32),
            pltpu.VMEM((HEADS + 1, RANK, HEAD_SIZE), f32),
            pltpu.VMEM((2, fresh, TOKENS), f32),
            pltpu.VMEM((2, fresh, TOKENS), f32),
            pltpu.VMEM((2, KEYS, TOKENS), bf),
            pltpu.VMEM((2, KEYS, TOKENS), bf),
        ],
        flops=2 * 4 * HEADS * TOKENS * KEYS * HEAD_SIZE,
    )(place, both, g, three, *packs, *ready)
    got = lax.all_gather(send, "core", axis=0, tiled=True)
    (sums,) = call(pair_kernel, [((RANK // 2, 2, 2, HALF), bf)], [SMEM] + [VMEM] * 2)(
        place, keep, got
    )
    sums = lax.all_to_all(sums.reshape(RANK, 2, HALF), ("z", "y", "seq"), 0, 0, tiled=True)
    up_query = query_up_gradients.reshape(SHARE * HEADS, HEAD_SIZE)
    up_value = value_up_gradients.reshape(SHARE, HEAD_SIZE)
    (lines,) = call(score_kernel, [((16, 1, LINE), f32)], [VMEM] * 3)(
        sums.reshape(RANK // 2, 2, 2, HALF), up_query, up_value
    )
    lines = lax.all_to_all(lines, ("z", "core"), 0, 0, tiled=True)
    (lines,) = call(relay_kernel, [((32, 1, LINE), f32)], [VMEM])(lines)
    lines = lax.all_to_all(lines, ("tp", "y", "seq"), 0, 0, tiled=True)
    (ranked,) = call(final_kernel, [((2, 2 * SHARE), f32)], [VMEM] * 2)(
        lines.reshape(16, 2, 1, LINE), query_ids.reshape(1, 2 * SHARE)
    )
    return ranked.T


def solution(mesh):
    fine = Mesh(mesh.devices.reshape(4, 8, 2, 4, 2), ("y", "z", "core", "tp", "seq"))
    split = P("seq", CTX, "tp")
    placed = (split, split, split, split, P("seq", CTX, None), P(), P(), P(), split, split)
    return jax.shard_map(body, mesh=fine, in_specs=placed, out_specs=P(), check_vma=False)
```

```python
import functools

import jax
import jax.numpy as jnp
from jax import lax
from jax.experimental import pallas as pl
from jax.experimental.pallas import tpu as pltpu
from jax.sharding import Mesh
from jax.sharding import PartitionSpec as P

HEAD_SIZE = 128
WINDOW_BLOCKS = 3
TOKENS = 256
RANK = 64
HEADS = 8
KEYS = (WINDOW_BLOCKS + 1) * TOKENS
FEATURES = HEADS * HEAD_SIZE + HEAD_SIZE
HALF = 640
PACK = 2 * TOKENS + 128
CHUNK = 64
CHUNKS = [slice(i * CHUNK, (i + 1) * CHUNK) for i in range(KEYS // CHUNK)]
EARLY = 2
SHARE = 256
LINE = 2 * SHARE + 128
NEG_FILL = -1e30
SCALE = HEAD_SIZE ** (-0.5)
LOG2E = 1.4426950408889634

CTX = ("y", "z", "core")
VMEM = pl.BlockSpec(memory_space=pltpu.VMEM)
SMEM = pl.BlockSpec(memory_space=pltpu.SMEM)
NT = (((1,), (1,)), ((), ()))


def lanes(head):
    return slice(head * HEAD_SIZE, (head + 1) * HEAD_SIZE)


def folded(x):
    return x.reshape(x.shape[0] // 8, 8, TOKENS)


def visible_bias(place, stop):
    row = lax.broadcasted_iota(jnp.int32, (TOKENS, TOKENS), 0)
    col = lax.broadcasted_iota(jnp.int32, (TOKENS, TOKENS), 1)
    block, length, reach = place[0:1, :], place[1:2, :], place[2:3, :]
    gap = col - row + stop * TOKENS
    key_pos = (block - stop) * TOKENS + row
    allowed = (gap >= 0) & (gap < reach) & (key_pos < length) & (key_pos >= 0)
    return jnp.where(allowed, 0.0, NEG_FILL)


def pack_kernel(in_ref, out_ref):
    out_ref[0 : 2 * TOKENS, :] = in_ref[0 : 2 * TOKENS, :]
    low = in_ref[2 * TOKENS : 3 * TOKENS, RANK:].astype(jnp.float32)
    low = jnp.concatenate([low[:128], low[128:]], axis=1)
    out_ref[2 * TOKENS :, :] = low.astype(jnp.bfloat16)


def own_kernel(
    spot, both, pack, weight_ref, dprob_ref, stat_ref, g_ref, place, bias, score_buf
):
    def entry(at):
        return jnp.broadcast_to(spot[0:1, at : at + 1], (1, TOKENS))

    second = entry(1) == 1
    length = jnp.where(second, entry(3), entry(2))
    place[0:1, :] = entry(0)
    place[1:2, :] = length
    place[2:3, :] = jnp.where(second, entry(5), entry(4))
    token = lax.broadcasted_iota(jnp.int32, (TOKENS, HEAD_SIZE), 0)
    live = entry(0)[:, :HEAD_SIZE] * TOKENS + token < length[:, :HEAD_SIZE]
    live = jnp.where(live, 1.0, 0.0).astype(jnp.bfloat16)
    for head in range(HEADS):
        g_ref[:, lanes(head)] = both[TOKENS : 2 * TOKENS, lanes(head)] * live
    block_kernel(0, place, both, g_ref, pack, weight_ref, dprob_ref, stat_ref, bias, score_buf)


def block_kernel(
    stop, place, queries, cotangent, pack, weight_ref, dprob_ref, stat_ref, bias, score_buf
):
    bias[...] = visible_bias(place, stop)

    def products(head):
        score_buf[head % 2] = lax.dot_general(
            pack[0:TOKENS, :], queries[0:TOKENS, lanes(head)], NT, preferred_element_type=jnp.float32
        )
        dprob_ref[head] = lax.dot_general(
            pack[TOKENS : 2 * TOKENS, :],
            cotangent[:, lanes(head)],
            NT,
            preferred_element_type=jnp.float32,
        )

    products(0)
    for head in range(HEADS):
        if head + 1 < HEADS:
            products(head + 1)
        side = head % 2
        top = jnp.full((8, TOKENS), -3e38, jnp.float32)
        for rows in CHUNKS[: TOKENS // CHUNK]:
            scores = score_buf[side, rows] * (SCALE * LOG2E) + bias[rows]
            score_buf[side, rows] = scores
            top = jnp.maximum(top, jnp.max(folded(scores), axis=0))
        top = jnp.max(top, axis=0, keepdims=True)
        total = jnp.zeros((8, TOKENS), jnp.float32)
        inner = jnp.zeros((8, TOKENS), jnp.float32)
        for rows in CHUNKS[: TOKENS // CHUNK]:
            weights = jnp.exp2(score_buf[side, rows] - top)
            weight_ref[head, rows] = weights
            total = total + jnp.sum(folded(weights), axis=0)
            inner = inner + jnp.sum(folded(weights * dprob_ref[head, rows]), axis=0)
        stat_ref[head, 0:1, :] = top
        stat_ref[head, 1:2, :] = jnp.sum(total, axis=0, keepdims=True)
        stat_ref[head, 2:3, :] = jnp.sum(inner, axis=0, keepdims=True)


def attention_kernel(early_count, *refs):
    place, queries, cotangent, low_ref = refs[:4]
    packs = refs[4:8]
    early = [refs[8 + 3 * i : 11 + 3 * i] for i in range(early_count)]
    (
        keep_ref, send_ref, keys, values, keys_t, low_t, bias, sums,
        score_buf, dprob_buf, prob_buf, dscore_buf,
    ) = refs[8 + 3 * early_count :]
    core = place[0:1, :] % 2
    near = 1 + 2 * core
    first = core[:, :HEAD_SIZE] == 0
    stops = (0, 2, near, 4 - near)
    for slot in range(WINDOW_BLOCKS + 1):
        pack = packs[slot]
        rows = pl.ds(slot * TOKENS, TOKENS)
        key_block = pack[0:TOKENS, :]
        if slot >= early_count:
            fresh = pl.ds((slot - early_count) * TOKENS, TOKENS)
            keys[fresh, :] = key_block
            values[fresh, :] = pack[TOKENS : 2 * TOKENS, :]
            bias[fresh, :] = visible_bias(place, stops[slot])
        keys_t[:, rows] = key_block.T
        low_pair = pack[2 * TOKENS : PACK, :].T
        low_t[:, slot * TOKENS : slot * TOKENS + 128] = low_pair[:RANK]
        low_t[:, slot * TOKENS + 128 : (slot + 1) * TOKENS] = low_pair[RANK:]
    to = lax.broadcasted_iota(jnp.int32, (RANK, RANK), 0)
    source = lax.broadcasted_iota(jnp.int32, (RANK, RANK), 1)
    order = (to % 4) * 16 + (to % 32) // 4 * 2 + to // 32
    order = jnp.where(source == order, 1.0, 0.0).astype(jnp.bfloat16)
    query_low = low_ref[2 * TOKENS : 3 * TOKENS, :].T[:RANK]
    query_low = jnp.dot(order, query_low, preferred_element_type=jnp.float32).astype(jnp.bfloat16)
    value_low = jnp.dot(order, low_t[...], preferred_element_type=jnp.float32).astype(jnp.bfloat16)
    offset = early_count * TOKENS
    fresh_chunks = CHUNKS[: (KEYS - offset) // CHUNK]

    def products(head):
        side = head % 2
        score_buf[side] = lax.dot_general(
            keys[...], queries[0:TOKENS, lanes(head)], NT, preferred_element_type=jnp.float32
        )
        dprob_buf[side] = lax.dot_general(
            values[...], cotangent[:, lanes(head)], NT, preferred_element_type=jnp.float32
        )

    def softmax(head):
        side = head % 2
        top = jnp.full((8, TOKENS), -3e38, jnp.float32)
        for rows in fresh_chunks:
            scores = score_buf[side, rows] * (SCALE * LOG2E) + bias[rows]
            score_buf[side, rows] = scores
            top = jnp.maximum(top, jnp.max(folded(scores), axis=0))
        top = jnp.max(top, axis=0, keepdims=True)
        for _, _, stat in early:
            top = jnp.maximum(top, stat[head, 0:1, :])
        total = jnp.zeros((8, TOKENS), jnp.float32)
        inner = jnp.zeros((8, TOKENS), jnp.float32)
        for rows in fresh_chunks:
            weights = jnp.exp2(score_buf[side, rows] - top)
            score_buf[side, rows] = weights
            total = total + jnp.sum(folded(weights), axis=0)
            inner = inner + jnp.sum(folded(weights * dprob_buf[side, rows]), axis=0)
        total = jnp.sum(total, axis=0, keepdims=True)
        inner = jnp.sum(inner, axis=0, keepdims=True)
        fades = []
        for _, _, stat in early:
            fade = jnp.exp2(stat[head, 0:1, :] - top)
            total = total + fade * stat[head, 1:2, :]
            inner = inner + fade * stat[head, 2:3, :]
            fades.append(fade)
        fraction = 1.0 / total
        inner = inner * fraction

        def settle(weights, dprob, factor, at):
            prob = weights * factor
            prob_buf[side, at : at + CHUNK] = prob.astype(jnp.bfloat16)
            dscore_buf[side, at : at + CHUNK] = (prob * (dprob - inner)).astype(jnp.bfloat16)

        for slot, (weight, dprob, _) in enumerate(early):
            factor = fades[slot] * fraction
            for rows in CHUNKS[: TOKENS // CHUNK]:
                settle(weight[head, rows], dprob[head, rows], factor, slot * TOKENS + rows.start)
        for rows in fresh_chunks:
            settle(score_buf[side, rows], dprob_buf[side, rows], fraction, offset + rows.start)

    def finish(head, value_sum):
        side = head % 2
        query_grad = jnp.dot(keys_t[...], dscore_buf[side], preferred_element_type=jnp.float32)
        query_grad = (query_grad * SCALE).astype(jnp.bfloat16)
        sums[head] = lax.dot_general(
            query_low, query_grad, NT, preferred_element_type=jnp.float32
        )
        g = cotangent[:, lanes(head)]
        return value_sum + jnp.dot(prob_buf[side], g, preferred_element_type=jnp.float32)

    value_sum = jnp.zeros((KEYS, HEAD_SIZE), jnp.float32)
    products(0)
    for head in range(HEADS):
        if head + 1 < HEADS:
            products(head + 1)
        if head > 0:
            value_sum = finish(head - 1, value_sum)
        softmax(head)
    value_sum = finish(HEADS - 1, value_sum)
    sums[HEADS] = jnp.dot(
        value_low, value_sum.astype(jnp.bfloat16), preferred_element_type=jnp.float32
    )
    for head in range(HEADS + 1):
        even = sums[head, 0:32, :]
        odd = sums[head, 32:64, :]
        keep_ref[:, lanes(head)] = jnp.where(first, even, odd)
        send_ref[:, lanes(head)] = jnp.where(first, odd, even)


def pair_kernel(place, keep_ref, got_ref, out_ref):
    rows = RANK // 2
    first = jnp.broadcast_to(place[0:1, :128] % 2 == 0, (rows, 128))
    first = jnp.concatenate([first] * (FEATURES // 128), axis=1)
    total = keep_ref[...] + jnp.where(first, got_ref[rows:, :], got_ref[:rows, :])
    upper = jnp.concatenate([total[:, HALF:], jnp.zeros((32, 2 * HALF - FEATURES))], axis=1)
    both = jnp.stack([total[:, :HALF], upper], axis=1).astype(jnp.bfloat16)
    for seq in range(2):
        out_ref[:, seq] = both


def score_kernel(rows_ref, up_query, up_value, out_ref):
    pieces = []
    squares = []
    for b in range(2):
        row = jnp.sum(rows_ref[:, b].astype(jnp.float32), axis=0)
        row = jnp.concatenate([row[0:1], row[1:2, : FEATURES - HALF]], axis=1)
        squares.append(jnp.sum(row * row))
        total = up_value[...] * row[:, HEADS * HEAD_SIZE :]
        for k in range(HEADS):
            total = total + up_query[pl.ds(k, SHARE, stride=HEADS), :] * row[
                :, k * HEAD_SIZE : (k + 1) * HEAD_SIZE
            ]
        pieces.append(jnp.sum(total.T, axis=0, keepdims=True))
    lane = lax.broadcasted_iota(jnp.int32, (1, 128), 1)
    tail = jnp.where(lane == 0, squares[0], jnp.where(lane == 1, squares[1], 0.0))
    line = jnp.concatenate(pieces + [tail], axis=1)
    for i in range(out_ref.shape[0]):
        out_ref[i] = line


def relay_kernel(in_ref, out_ref):
    line = jnp.sum(in_ref[...], axis=0)
    for i in range(out_ref.shape[0]):
        out_ref[i] = line


def final_kernel(in_ref, ids_ref, out_ref):
    halves = [jnp.sum(in_ref[:, s], axis=0) for s in range(2)]
    count = 2 * SHARE
    rest = []
    for b in range(2):
        square = halves[0][:, count + b : count + b + 1]
        part = [half[:, b * SHARE : (b + 1) * SHARE] for half in halves]
        scores = jnp.concatenate(part, axis=1) / jnp.sqrt(square + 1e-06)
        rest.append(scores)
    slot = lax.broadcasted_iota(jnp.int32, (count, count), 0)
    chosen = jnp.where(slot == ids_ref[...], 1.0, 0.0).astype(jnp.bfloat16)
    left = jnp.concatenate(rest, axis=0)
    pieces = []
    for _ in range(3):
        piece = left.astype(jnp.bfloat16)
        left = left - piece.astype(jnp.float32)
        pieces.append(piece.astype(jnp.float32))
    pieces.append(jnp.zeros((2, count), jnp.float32))
    stack = jnp.concatenate(pieces, axis=0).astype(jnp.bfloat16)
    total = jnp.dot(stack, chosen, preferred_element_type=jnp.float32)
    out_ref[...] = total[0:2] + total[2:4] + total[4:6]


def call(kernel, made, specs, scratch=(), flops=0, out_specs=None):
    return pl.pallas_call(
        kernel,
        out_shape=[jax.ShapeDtypeStruct(*one) for one in made],
        in_specs=specs,
        out_specs=out_specs or [VMEM] * len(made),
        scratch_shapes=list(scratch),
        compiler_params=pltpu.CompilerParams(vmem_limit_bytes=32 * 2**20),
        cost_estimate=pl.CostEstimate(flops=flops, bytes_accessed=2**20, transcendentals=0),
    )


def body(
    queries, attention_keys, attention_values, cotangent, low_rank, seq_lengths,
    window_stops, query_ids, query_up_gradients, value_up_gradients,
):
    bf, f32 = jnp.bfloat16, jnp.float32
    three = jnp.concatenate([attention_keys[0], attention_values[0], low_rank[0]], axis=0)
    (pack,) = call(pack_kernel, [((PACK, HEAD_SIZE), bf)], [VMEM])(three)
    count = 64
    early = lax.ppermute(pack, CTX, [(i, i + 2) for i in range(count - 2)])
    apart = [(i, i + 1 + 2 * (i % 2)) for i in range(count) if i + 1 + 2 * (i % 2) < count]
    spot = jnp.stack([lax.axis_index(CTX), lax.axis_index("seq")]).astype(jnp.int32)
    spot = jnp.concatenate([spot, seq_lengths, window_stops])
    both = jnp.concatenate([queries[0], cotangent[0]], axis=0)
    later, both = lax.optimization_barrier((pack, both))
    far = lax.ppermute(later, CTX, apart)
    tile = (TOKENS, TOKENS)
    scored = [((HEADS, *tile), f32), ((HEADS, *tile), f32), ((HEADS, 8, TOKENS), f32)]
    scratch = [pltpu.VMEM(tile, f32), pltpu.VMEM((2, *tile), f32)]
    flops = 2 * 2 * HEADS * TOKENS * TOKENS * HEAD_SIZE
    row = ((TOKENS, HEADS * HEAD_SIZE), bf)
    *own, g, place = call(
        own_kernel, scored + [row, ((8, TOKENS), jnp.int32)],
        [VMEM] * 3, scratch, flops,
    )(spot.reshape(1, 6), both, pack)
    early, own[2] = lax.optimization_barrier((early, own[2]))
    other = lax.ppermute(early, "core", [(0, 1), (1, 0)])
    near = call(
        functools.partial(block_kernel, 2), scored, [VMEM] * 4, scratch, flops
    )(place, both, g, early)
    ready = [*own, *near]
    packs = [pack, early, other, far]
    fresh = KEYS - EARLY * TOKENS
    keep, send = call(
        functools.partial(attention_kernel, EARLY), [((RANK // 2, FEATURES), f32)] * 2,
        [VMEM] * (8 + 3 * EARLY),
        [
            pltpu.VMEM((fresh, HEAD_SIZE), bf),
            pltpu.VMEM((fresh, HEAD_SIZE), bf),
            pltpu.VMEM((HEAD_SIZE, KEYS), bf),
            pltpu.VMEM((RANK, KEYS), bf),
            pltpu.VMEM((fresh, TOKENS), f32),
            pltpu.VMEM((HEADS + 1, RANK, HEAD_SIZE), f32),
            pltpu.VMEM((2, fresh, TOKENS), f32),
            pltpu.VMEM((2, fresh, TOKENS), f32),
            pltpu.VMEM((2, KEYS, TOKENS), bf),
            pltpu.VMEM((2, KEYS, TOKENS), bf),
        ],
        flops=2 * 4 * HEADS * TOKENS * KEYS * HEAD_SIZE,
    )(place, both, g, three, *packs, *ready)
    got = lax.all_gather(send, "core", axis=0, tiled=True)
    (sums,) = call(pair_kernel, [((RANK // 2, 2, 2, HALF), bf)], [VMEM] * 3)(
        place, keep, got
    )
    sums = lax.all_to_all(sums.reshape(RANK, 2, HALF), ("z", "y", "seq"), 0, 0, tiled=True)
    up_query = query_up_gradients.reshape(SHARE * HEADS, HEAD_SIZE)
    up_value = value_up_gradients.reshape(SHARE, HEAD_SIZE)
    (lines,) = call(score_kernel, [((16, 1, LINE), f32)], [VMEM] * 3)(
        sums.reshape(RANK // 2, 2, 2, HALF), up_query, up_value
    )
    lines = lax.all_to_all(lines, ("z", "core"), 0, 0, tiled=True)
    (lines,) = call(relay_kernel, [((32, 1, LINE), f32)], [VMEM])(lines)
    lines = lax.all_to_all(lines, ("tp", "y", "seq"), 0, 0, tiled=True)
    (ranked,) = call(final_kernel, [((2, 2 * SHARE), f32)], [VMEM] * 2)(
        lines.reshape(16, 2, 1, LINE), query_ids.reshape(1, 2 * SHARE)
    )
    return ranked.T


def solution(mesh):
    fine = Mesh(mesh.devices.reshape(4, 8, 2, 4, 2), ("y", "z", "core", "tp", "seq"))
    split = P("seq", CTX, "tp")
    placed = (split, split, split, split, P("seq", CTX, None), P(), P(), P(), split, split)
    return jax.shard_map(body, mesh=fine, in_specs=placed, out_specs=P(), check_vma=False)
```

```python
import functools

import jax
import jax.numpy as jnp
from jax import lax
from jax.experimental import pallas as pl
from jax.experimental.pallas import tpu as pltpu
from jax.sharding import Mesh
from jax.sharding import PartitionSpec as P

HEAD_SIZE = 128
WINDOW_BLOCKS = 3
TOKENS = 256
RANK = 64
HEADS = 8
KEYS = (WINDOW_BLOCKS + 1) * TOKENS
FEATURES = HEADS * HEAD_SIZE + HEAD_SIZE
HALF = 640
PACK = 2 * TOKENS + 128
CHUNK = 64
CHUNKS = [slice(i * CHUNK, (i + 1) * CHUNK) for i in range(KEYS // CHUNK)]
EARLY = 2
SHARE = 256
LINE = 2 * SHARE + 128
NEG_FILL = -1e30
SCALE = HEAD_SIZE ** (-0.5)
LOG2E = 1.4426950408889634

CTX = ("y", "z", "core")
VMEM = pl.BlockSpec(memory_space=pltpu.VMEM)
SMEM = pl.BlockSpec(memory_space=pltpu.SMEM)
NT = (((1,), (1,)), ((), ()))


def lanes(head):
    return slice(head * HEAD_SIZE, (head + 1) * HEAD_SIZE)


def folded(x):
    return x.reshape(x.shape[0] // 8, 8, TOKENS)


def visible_bias(place, stop):
    row = lax.broadcasted_iota(jnp.int32, (TOKENS, TOKENS), 0)
    col = lax.broadcasted_iota(jnp.int32, (TOKENS, TOKENS), 1)
    block, length, reach = place[0:1, :], place[1:2, :], place[2:3, :]
    gap = col - row + stop * TOKENS
    key_pos = (block - stop) * TOKENS + row
    allowed = (gap >= 0) & (gap < reach) & (key_pos < length) & (key_pos >= 0)
    return jnp.where(allowed, 0.0, NEG_FILL)


def pack_kernel(in_ref, out_ref):
    out_ref[0 : 2 * TOKENS, :] = in_ref[0 : 2 * TOKENS, :]
    low = in_ref[2 * TOKENS : 3 * TOKENS, RANK:].astype(jnp.float32)
    low = jnp.concatenate([low[:128], low[128:]], axis=1)
    out_ref[2 * TOKENS :, :] = low.astype(jnp.bfloat16)


def row_order():
    to = lax.broadcasted_iota(jnp.int32, (RANK, RANK), 0)
    source = lax.broadcasted_iota(jnp.int32, (RANK, RANK), 1)
    order = (to % 4) * 16 + (to % 32) // 4 * 2 + to // 32
    return jnp.where(source == order, 1.0, 0.0).astype(jnp.bfloat16)


def ordered(low):
    low = jnp.dot(row_order(), low, preferred_element_type=jnp.float32)
    return low.astype(jnp.bfloat16)


def value_low(pack):
    low = pack[2 * TOKENS : PACK, :].T
    return ordered(jnp.concatenate([low[:RANK], low[RANK:]], axis=1))


def own_kernel(spot, both, pack, low_ref, *refs):
    g_ref, place, query_low = refs[5:8]
    query_low[...] = ordered(low_ref[2 * TOKENS : 3 * TOKENS, :].T[:RANK])

    def entry(at):
        return jnp.broadcast_to(spot[0:1, at : at + 1], (1, TOKENS))

    second = entry(1) == 1
    length = jnp.where(second, entry(3), entry(2))
    place[0:1, :] = entry(0)
    place[1:2, :] = length
    place[2:3, :] = jnp.where(second, entry(5), entry(4))
    token = lax.broadcasted_iota(jnp.int32, (TOKENS, HEAD_SIZE), 0)
    live = entry(0)[:, :HEAD_SIZE] * TOKENS + token < length[:, :HEAD_SIZE]
    live = jnp.where(live, 1.0, 0.0).astype(jnp.bfloat16)
    for head in range(HEADS):
        g_ref[:, lanes(head)] = both[TOKENS : 2 * TOKENS, lanes(head)] * live
    block_kernel(0, place, both, g_ref, pack, *refs[:5], *refs[8:])


def block_kernel(
    stop, place, queries, cotangent, pack,
    weight_ref, dprob_ref, stat_ref, key_t, low_t, bias, score_buf,
):
    bias[...] = visible_bias(place, stop)
    key_t[...] = pack[0:TOKENS, :].T
    low_t[...] = value_low(pack)

    def products(head):
        score_buf[head % 2] = lax.dot_general(
            pack[0:TOKENS, :], queries[0:TOKENS, lanes(head)], NT, preferred_element_type=jnp.float32
        )
        dprob_ref[head] = lax.dot_general(
            pack[TOKENS : 2 * TOKENS, :],
            cotangent[:, lanes(head)],
            NT,
            preferred_element_type=jnp.float32,
        )

    products(0)
    for head in range(HEADS):
        if head + 1 < HEADS:
            products(head + 1)
        side = head % 2
        top = jnp.full((8, TOKENS), -3e38, jnp.float32)
        for rows in CHUNKS[: TOKENS // CHUNK]:
            scores = score_buf[side, rows] * (SCALE * LOG2E) + bias[rows]
            score_buf[side, rows] = scores
            top = jnp.maximum(top, jnp.max(folded(scores), axis=0))
        top = jnp.max(top, axis=0, keepdims=True)
        total = jnp.zeros((8, TOKENS), jnp.float32)
        inner = jnp.zeros((8, TOKENS), jnp.float32)
        for rows in CHUNKS[: TOKENS // CHUNK]:
            weights = jnp.exp2(score_buf[side, rows] - top)
            weight_ref[head, rows] = weights
            total = total + jnp.sum(folded(weights), axis=0)
            inner = inner + jnp.sum(folded(weights * dprob_ref[head, rows]), axis=0)
        stat_ref[head, 0:1, :] = top
        stat_ref[head, 1:2, :] = jnp.sum(total, axis=0, keepdims=True)
        stat_ref[head, 2:3, :] = jnp.sum(inner, axis=0, keepdims=True)


def attention_kernel(early_count, *refs):
    place, queries, cotangent, query_low = refs[:4]
    packs = refs[4:8]
    early = [refs[8 + 5 * i : 13 + 5 * i] for i in range(early_count)]
    (
        keep_ref, send_ref, keys, values, keys_t, low_t, bias, sums,
        score_buf, dprob_buf, prob_buf, dscore_buf,
    ) = refs[8 + 5 * early_count :]
    core = place[0:1, :] % 2
    near = 1 + 2 * core
    first = core[:, :HEAD_SIZE] == 0
    stops = (0, 2, near, 4 - near)
    for slot in range(WINDOW_BLOCKS + 1):
        pack = packs[slot]
        rows = pl.ds(slot * TOKENS, TOKENS)
        if slot < early_count:
            keys_t[:, rows] = early[slot][3][...]
            low_t[:, rows] = early[slot][4][...]
        else:
            key_block = pack[0:TOKENS, :]
            fresh = pl.ds((slot - early_count) * TOKENS, TOKENS)
            keys[fresh, :] = key_block
            values[fresh, :] = pack[TOKENS : 2 * TOKENS, :]
            bias[fresh, :] = visible_bias(place, stops[slot])
            keys_t[:, rows] = key_block.T
            low_t[:, rows] = value_low(pack)
    offset = early_count * TOKENS
    fresh_chunks = CHUNKS[: (KEYS - offset) // CHUNK]

    def products(head):
        side = head % 2
        score_buf[side] = lax.dot_general(
            keys[...], queries[0:TOKENS, lanes(head)], NT, preferred_element_type=jnp.float32
        )
        dprob_buf[side] = lax.dot_general(
            values[...], cotangent[:, lanes(head)], NT, preferred_element_type=jnp.float32
        )

    def softmax(head):
        side = head % 2
        top = jnp.full((8, TOKENS), -3e38, jnp.float32)
        for rows in fresh_chunks:
            scores = score_buf[side, rows] * (SCALE * LOG2E) + bias[rows]
            score_buf[side, rows] = scores
            top = jnp.maximum(top, jnp.max(folded(scores), axis=0))
        top = jnp.max(top, axis=0, keepdims=True)
        for _, _, stat, _, _ in early:
            top = jnp.maximum(top, stat[head, 0:1, :])
        total = jnp.zeros((8, TOKENS), jnp.float32)
        inner = jnp.zeros((8, TOKENS), jnp.float32)
        for rows in fresh_chunks:
            weights = jnp.exp2(score_buf[side, rows] - top)
            score_buf[side, rows] = weights
            total = total + jnp.sum(folded(weights), axis=0)
            inner = inner + jnp.sum(folded(weights * dprob_buf[side, rows]), axis=0)
        total = jnp.sum(total, axis=0, keepdims=True)
        inner = jnp.sum(inner, axis=0, keepdims=True)
        fades = []
        for _, _, stat, _, _ in early:
            fade = jnp.exp2(stat[head, 0:1, :] - top)
            total = total + fade * stat[head, 1:2, :]
            inner = inner + fade * stat[head, 2:3, :]
            fades.append(fade)
        fraction = 1.0 / total
        inner = inner * fraction

        def settle(weights, dprob, factor, at):
            prob = weights * factor
            prob_buf[side, at : at + CHUNK] = prob.astype(jnp.bfloat16)
            dscore_buf[side, at : at + CHUNK] = (prob * (dprob - inner)).astype(jnp.bfloat16)

        for slot, (weight, dprob, *_) in enumerate(early):
            factor = fades[slot] * fraction
            for rows in CHUNKS[: TOKENS // CHUNK]:
                settle(weight[head, rows], dprob[head, rows], factor, slot * TOKENS + rows.start)
        for rows in fresh_chunks:
            settle(score_buf[side, rows], dprob_buf[side, rows], fraction, offset + rows.start)

    def finish(head, value_sum):
        side = head % 2
        query_grad = jnp.dot(keys_t[...], dscore_buf[side], preferred_element_type=jnp.float32)
        query_grad = (query_grad * SCALE).astype(jnp.bfloat16)
        sums[head] = lax.dot_general(
            query_low[...], query_grad, NT, preferred_element_type=jnp.float32
        )
        g = cotangent[:, lanes(head)]
        return value_sum + jnp.dot(prob_buf[side], g, preferred_element_type=jnp.float32)

    value_sum = jnp.zeros((KEYS, HEAD_SIZE), jnp.float32)
    products(0)
    for head in range(HEADS):
        if head + 1 < HEADS:
            products(head + 1)
        if head > 0:
            value_sum = finish(head - 1, value_sum)
        softmax(head)
    value_sum = finish(HEADS - 1, value_sum)
    sums[HEADS] = jnp.dot(
        low_t[...], value_sum.astype(jnp.bfloat16), preferred_element_type=jnp.float32
    )
    for head in range(HEADS + 1):
        even = sums[head, 0:32, :]
        odd = sums[head, 32:64, :]
        keep_ref[:, lanes(head)] = jnp.where(first, even, odd)
        send_ref[:, lanes(head)] = jnp.where(first, odd, even)


def pair_kernel(place, keep_ref, got_ref, out_ref):
    rows = RANK // 2
    first = jnp.broadcast_to(place[0:1, :128] % 2 == 0, (rows, 128))
    first = jnp.concatenate([first] * (FEATURES // 128), axis=1)
    total = keep_ref[...] + jnp.where(first, got_ref[rows:, :], got_ref[:rows, :])
    upper = jnp.concatenate([total[:, HALF:], jnp.zeros((32, 2 * HALF - FEATURES))], axis=1)
    both = jnp.stack([total[:, :HALF], upper], axis=1).astype(jnp.bfloat16)
    for seq in range(2):
        out_ref[:, seq] = both


def score_kernel(rows_ref, up_query, up_value, out_ref):
    pieces = []
    squares = []
    for b in range(2):
        row = jnp.sum(rows_ref[:, b].astype(jnp.float32), axis=0)
        row = jnp.concatenate([row[0:1], row[1:2, : FEATURES - HALF]], axis=1)
        squares.append(jnp.sum(row * row))
        total = up_value[...] * row[:, HEADS * HEAD_SIZE :]
        for k in range(HEADS):
            total = total + up_query[pl.ds(k, SHARE, stride=HEADS), :] * row[
                :, k * HEAD_SIZE : (k + 1) * HEAD_SIZE
            ]
        pieces.append(jnp.sum(total.T, axis=0, keepdims=True))
    lane = lax.broadcasted_iota(jnp.int32, (1, 128), 1)
    tail = jnp.where(lane == 0, squares[0], jnp.where(lane == 1, squares[1], 0.0))
    line = jnp.concatenate(pieces + [tail], axis=1)
    for i in range(out_ref.shape[0]):
        out_ref[i] = line


def relay_kernel(in_ref, out_ref):
    line = jnp.sum(in_ref[...], axis=0)
    for i in range(out_ref.shape[0]):
        out_ref[i] = line


def final_kernel(in_ref, ids_ref, out_ref):
    halves = [jnp.sum(in_ref[:, s], axis=0) for s in range(2)]
    count = 2 * SHARE
    rest = []
    for b in range(2):
        square = halves[0][:, count + b : count + b + 1]
        part = [half[:, b * SHARE : (b + 1) * SHARE] for half in halves]
        scores = jnp.concatenate(part, axis=1) / jnp.sqrt(square + 1e-06)
        rest.append(scores)
    slot = lax.broadcasted_iota(jnp.int32, (count, count), 0)
    chosen = jnp.where(slot == ids_ref[...], 1.0, 0.0).astype(jnp.bfloat16)
    left = jnp.concatenate(rest, axis=0)
    pieces = []
    for _ in range(3):
        piece = left.astype(jnp.bfloat16)
        left = left - piece.astype(jnp.float32)
        pieces.append(piece.astype(jnp.float32))
    pieces.append(jnp.zeros((2, count), jnp.float32))
    stack = jnp.concatenate(pieces, axis=0).astype(jnp.bfloat16)
    total = jnp.dot(stack, chosen, preferred_element_type=jnp.float32)
    out_ref[...] = total[0:2] + total[2:4] + total[4:6]


def call(kernel, made, specs, scratch=(), flops=0, out_specs=None):
    return pl.pallas_call(
        kernel,
        out_shape=[jax.ShapeDtypeStruct(*one) for one in made],
        in_specs=specs,
        out_specs=out_specs or [VMEM] * len(made),
        scratch_shapes=list(scratch),
        compiler_params=pltpu.CompilerParams(vmem_limit_bytes=32 * 2**20),
        cost_estimate=pl.CostEstimate(flops=flops, bytes_accessed=2**20, transcendentals=0),
    )


def body(
    queries, attention_keys, attention_values, cotangent, low_rank, seq_lengths,
    window_stops, query_ids, query_up_gradients, value_up_gradients,
):
    bf, f32 = jnp.bfloat16, jnp.float32
    three = jnp.concatenate([attention_keys[0], attention_values[0], low_rank[0]], axis=0)
    (pack,) = call(pack_kernel, [((PACK, HEAD_SIZE), bf)], [VMEM])(three)
    count = 64
    early = lax.ppermute(pack, CTX, [(i, i + 2) for i in range(count - 2)])
    apart = [(i, i + 1 + 2 * (i % 2)) for i in range(count) if i + 1 + 2 * (i % 2) < count]
    spot = jnp.stack([lax.axis_index(CTX), lax.axis_index("seq")]).astype(jnp.int32)
    spot = jnp.concatenate([spot, seq_lengths, window_stops])
    both = jnp.concatenate([queries[0], cotangent[0]], axis=0)
    later, both = lax.optimization_barrier((pack, both))
    far = lax.ppermute(later, CTX, apart)
    tile = (TOKENS, TOKENS)
    scored = [((HEADS, *tile), f32), ((HEADS, *tile), f32), ((HEADS, 8, TOKENS), f32)]
    scored += [((HEAD_SIZE, TOKENS), bf), ((RANK, TOKENS), bf)]
    scratch = [pltpu.VMEM(tile, f32), pltpu.VMEM((2, *tile), f32)]
    flops = 2 * 2 * HEADS * TOKENS * TOKENS * HEAD_SIZE
    row = ((TOKENS, HEADS * HEAD_SIZE), bf)
    *own, g, place, turned = call(
        own_kernel, scored + [row, ((8, TOKENS), jnp.int32), ((RANK, TOKENS), bf)],
        [VMEM] * 4, scratch, flops,
    )(spot.reshape(1, 6), both, pack, three)
    early, own[2] = lax.optimization_barrier((early, own[2]))
    other = lax.ppermute(early, "core", [(0, 1), (1, 0)])
    near = call(
        functools.partial(block_kernel, 2), scored, [VMEM] * 4, scratch, flops
    )(place, both, g, early)
    ready = [*own, *near]
    packs = [pack, early, other, far]
    fresh = KEYS - EARLY * TOKENS
    keep, send = call(
        functools.partial(attention_kernel, EARLY), [((RANK // 2, FEATURES), f32)] * 2,
        [VMEM] * (8 + 5 * EARLY),
        [
            pltpu.VMEM((fresh, HEAD_SIZE), bf),
            pltpu.VMEM((fresh, HEAD_SIZE), bf),
            pltpu.VMEM((HEAD_SIZE, KEYS), bf),
            pltpu.VMEM((RANK, KEYS), bf),
            pltpu.VMEM((fresh, TOKENS), f32),
            pltpu.VMEM((HEADS + 1, RANK, HEAD_SIZE), f32),
            pltpu.VMEM((2, fresh, TOKENS), f32),
            pltpu.VMEM((2, fresh, TOKENS), f32),
            pltpu.VMEM((2, KEYS, TOKENS), bf),
            pltpu.VMEM((2, KEYS, TOKENS), bf),
        ],
        flops=2 * 4 * HEADS * TOKENS * KEYS * HEAD_SIZE,
    )(place, both, g, turned, *packs, *ready)
    got = lax.all_gather(send, "core", axis=0, tiled=True)
    (sums,) = call(pair_kernel, [((RANK // 2, 2, 2, HALF), bf)], [VMEM] * 3)(
        place, keep, got
    )
    sums = lax.all_to_all(sums.reshape(RANK, 2, HALF), ("z", "y", "seq"), 0, 0, tiled=True)
    up_query = query_up_gradients.reshape(SHARE * HEADS, HEAD_SIZE)
    up_value = value_up_gradients.reshape(SHARE, HEAD_SIZE)
    (lines,) = call(score_kernel, [((16, 1, LINE), f32)], [VMEM] * 3)(
        sums.reshape(RANK // 2, 2, 2, HALF), up_query, up_value
    )
    lines = lax.all_to_all(lines, ("z", "core"), 0, 0, tiled=True)
    (lines,) = call(relay_kernel, [((32, 1, LINE), f32)], [VMEM])(lines)
    lines = lax.all_to_all(lines, ("tp", "y", "seq"), 0, 0, tiled=True)
    (ranked,) = call(final_kernel, [((2, 2 * SHARE), f32)], [VMEM] * 2)(
        lines.reshape(16, 2, 1, LINE), query_ids.reshape(1, 2 * SHARE)
    )
    return ranked.T


def solution(mesh):
    fine = Mesh(mesh.devices.reshape(4, 8, 2, 4, 2), ("y", "z", "core", "tp", "seq"))
    split = P("seq", CTX, "tp")
    placed = (split, split, split, split, P("seq", CTX, None), P(), P(), P(), split, split)
    return jax.shard_map(body, mesh=fine, in_specs=placed, out_specs=P(), check_vma=False)
```

```python
import functools

import jax
import jax.numpy as jnp
from jax import lax
from jax.experimental import pallas as pl
from jax.experimental.pallas import tpu as pltpu
from jax.sharding import Mesh
from jax.sharding import PartitionSpec as P

HEAD_SIZE = 128
WINDOW_BLOCKS = 3
TOKENS = 256
RANK = 64
HEADS = 8
KEYS = (WINDOW_BLOCKS + 1) * TOKENS
FEATURES = HEADS * HEAD_SIZE + HEAD_SIZE
HALF = 640
PACK = 2 * TOKENS + 128
CHUNK = 64
CHUNKS = [slice(i * CHUNK, (i + 1) * CHUNK) for i in range(KEYS // CHUNK)]
EARLY = 2
SHARE = 256
LINE = 2 * SHARE + 128
NEG_FILL = -1e30
SCALE = HEAD_SIZE ** (-0.5)
LOG2E = 1.4426950408889634

CTX = ("y", "z", "core")
VMEM = pl.BlockSpec(memory_space=pltpu.VMEM)
SMEM = pl.BlockSpec(memory_space=pltpu.SMEM)
NT = (((1,), (1,)), ((), ()))


def lanes(head):
    return slice(head * HEAD_SIZE, (head + 1) * HEAD_SIZE)


def folded(x):
    return x.reshape(x.shape[0] // 8, 8, TOKENS)


def visible_bias(place, stop):
    row = lax.broadcasted_iota(jnp.int32, (TOKENS, TOKENS), 0)
    col = lax.broadcasted_iota(jnp.int32, (TOKENS, TOKENS), 1)
    block, length, reach = place[0:1, :], place[1:2, :], place[2:3, :]
    gap = col - row + stop * TOKENS
    key_pos = (block - stop) * TOKENS + row
    allowed = (gap >= 0) & (gap < reach) & (key_pos < length) & (key_pos >= 0)
    return jnp.where(allowed, 0.0, NEG_FILL)


def pack_kernel(in_ref, out_ref):
    out_ref[0 : 2 * TOKENS, :] = in_ref[0 : 2 * TOKENS, :]
    low = in_ref[2 * TOKENS : 3 * TOKENS, RANK:].astype(jnp.float32)
    low = jnp.concatenate([low[:128], low[128:]], axis=1)
    out_ref[2 * TOKENS :, :] = low.astype(jnp.bfloat16)


def own_kernel(
    spot, both, pack, weight_ref, dprob_ref, stat_ref, g_ref, place, bias, score_buf
):
    def entry(at):
        return jnp.broadcast_to(spot[0:1, at : at + 1], (1, TOKENS))

    second = entry(1) == 1
    length = jnp.where(second, entry(3), entry(2))
    place[0:1, :] = entry(0)
    place[1:2, :] = length
    place[2:3, :] = jnp.where(second, entry(5), entry(4))
    token = lax.broadcasted_iota(jnp.int32, (TOKENS, HEAD_SIZE), 0)
    live = entry(0)[:, :HEAD_SIZE] * TOKENS + token < length[:, :HEAD_SIZE]
    live = jnp.where(live, 1.0, 0.0).astype(jnp.bfloat16)
    for head in range(HEADS):
        g_ref[:, lanes(head)] = both[TOKENS : 2 * TOKENS, lanes(head)] * live
    block_kernel(0, place, both, g_ref, pack, weight_ref, dprob_ref, stat_ref, bias, score_buf)


def block_kernel(
    stop, place, queries, cotangent, pack, weight_ref, dprob_ref, stat_ref, bias, score_buf
):
    bias[...] = visible_bias(place, stop)

    def products(head):
        score_buf[head % 2] = lax.dot_general(
            pack[0:TOKENS, :], queries[0:TOKENS, lanes(head)], NT, preferred_element_type=jnp.float32
        )
        dprob_ref[head] = lax.dot_general(
            pack[TOKENS : 2 * TOKENS, :],
            cotangent[:, lanes(head)],
            NT,
            preferred_element_type=jnp.float32,
        )

    products(0)
    for head in range(HEADS):
        if head + 1 < HEADS:
            products(head + 1)
        side = head % 2
        top = jnp.full((8, TOKENS), -3e38, jnp.float32)
        for rows in CHUNKS[: TOKENS // CHUNK]:
            scores = score_buf[side, rows] * (SCALE * LOG2E) + bias[rows]
            score_buf[side, rows] = scores
            top = jnp.maximum(top, jnp.max(folded(scores), axis=0))
        top = jnp.max(top, axis=0, keepdims=True)
        total = jnp.zeros((8, TOKENS), jnp.float32)
        inner = jnp.zeros((8, TOKENS), jnp.float32)
        for rows in CHUNKS[: TOKENS // CHUNK]:
            weights = jnp.exp2(score_buf[side, rows] - top)
            weight_ref[head, rows] = weights
            total = total + jnp.sum(folded(weights), axis=0)
            inner = inner + jnp.sum(folded(weights * dprob_ref[head, rows]), axis=0)
        stat_ref[head, 0:1, :] = top
        stat_ref[head, 1:2, :] = jnp.sum(total, axis=0, keepdims=True)
        stat_ref[head, 2:3, :] = jnp.sum(inner, axis=0, keepdims=True)


def attention_kernel(early_count, *refs):
    place, queries, cotangent, low_ref = refs[:4]
    packs = refs[4:8]
    early = [refs[8 + 3 * i : 11 + 3 * i] for i in range(early_count)]
    (
        keep_ref, send_ref, keys, values, keys_t, low_t, bias, sums,
        score_buf, dprob_buf, prob_buf, dscore_buf,
    ) = refs[8 + 3 * early_count :]
    core = place[0:1, :] % 2
    near = 1 + 2 * core
    first = core[:, :HEAD_SIZE] == 0
    stops = (0, 2, near, 4 - near)
    for slot in range(WINDOW_BLOCKS + 1):
        pack = packs[slot]
        rows = pl.ds(slot * TOKENS, TOKENS)
        key_block = pack[0:TOKENS, :]
        if slot >= early_count:
            fresh = pl.ds((slot - early_count) * TOKENS, TOKENS)
            keys[fresh, :] = key_block
            values[fresh, :] = pack[TOKENS : 2 * TOKENS, :]
            bias[fresh, :] = visible_bias(place, stops[slot])
        keys_t[:, rows] = key_block.T
        low_pair = pack[2 * TOKENS : PACK, :].T
        low_t[:, slot * TOKENS : slot * TOKENS + 128] = low_pair[:RANK]
        low_t[:, slot * TOKENS + 128 : (slot + 1) * TOKENS] = low_pair[RANK:]
    to = lax.broadcasted_iota(jnp.int32, (RANK, RANK), 0)
    source = lax.broadcasted_iota(jnp.int32, (RANK, RANK), 1)
    order = (to % 4) * 16 + (to % 32) // 4 * 2 + to // 32
    order = jnp.where(source == order, 1.0, 0.0).astype(jnp.bfloat16)
    query_low = low_ref[2 * TOKENS : 3 * TOKENS, :].T[:RANK]
    query_low = jnp.dot(order, query_low, preferred_element_type=jnp.float32).astype(jnp.bfloat16)
    value_low = jnp.dot(order, low_t[...], preferred_element_type=jnp.float32).astype(jnp.bfloat16)
    offset = early_count * TOKENS
    fresh_chunks = CHUNKS[: (KEYS - offset) // CHUNK]

    def products(head):
        side = head % 2
        score_buf[side] = lax.dot_general(
            keys[...], queries[0:TOKENS, lanes(head)], NT, preferred_element_type=jnp.float32
        )
        dprob_buf[side] = lax.dot_general(
            values[...], cotangent[:, lanes(head)], NT, preferred_element_type=jnp.float32
        )

    def softmax(head):
        side = head % 2
        top = jnp.full((8, TOKENS), -3e38, jnp.float32)
        for rows in fresh_chunks:
            scores = score_buf[side, rows] * (SCALE * LOG2E) + bias[rows]
            score_buf[side, rows] = scores
            top = jnp.maximum(top, jnp.max(folded(scores), axis=0))
        top = jnp.max(top, axis=0, keepdims=True)
        for _, _, stat in early:
            top = jnp.maximum(top, stat[head, 0:1, :])
        total = jnp.zeros((8, TOKENS), jnp.float32)
        inner = jnp.zeros((8, TOKENS), jnp.float32)
        for rows in fresh_chunks:
            weights = jnp.exp2(score_buf[side, rows] - top)
            score_buf[side, rows] = weights
            total = total + jnp.sum(folded(weights), axis=0)
            inner = inner + jnp.sum(folded(weights * dprob_buf[side, rows]), axis=0)
        total = jnp.sum(total, axis=0, keepdims=True)
        inner = jnp.sum(inner, axis=0, keepdims=True)
        fades = []
        for _, _, stat in early:
            fade = jnp.exp2(stat[head, 0:1, :] - top)
            total = total + fade * stat[head, 1:2, :]
            inner = inner + fade * stat[head, 2:3, :]
            fades.append(fade)
        fraction = 1.0 / total
        inner = inner * fraction

        def settle(weights, dprob, factor, at):
            prob = weights * factor
            prob_buf[side, at : at + CHUNK] = prob.astype(jnp.bfloat16)
            dscore_buf[side, at : at + CHUNK] = (prob * (dprob - inner)).astype(jnp.bfloat16)

        for slot, (weight, dprob, _) in enumerate(early):
            factor = fades[slot] * fraction
            for rows in CHUNKS[: TOKENS // CHUNK]:
                settle(weight[head, rows], dprob[head, rows], factor, slot * TOKENS + rows.start)
        for rows in fresh_chunks:
            settle(score_buf[side, rows], dprob_buf[side, rows], fraction, offset + rows.start)

    def finish(head, value_sum):
        side = head % 2
        query_grad = jnp.dot(keys_t[...], dscore_buf[side], preferred_element_type=jnp.float32)
        query_grad = (query_grad * SCALE).astype(jnp.bfloat16)
        sums[head] = lax.dot_general(
            query_low, query_grad, NT, preferred_element_type=jnp.float32
        )
        g = cotangent[:, lanes(head)]
        return value_sum + jnp.dot(prob_buf[side], g, preferred_element_type=jnp.float32)

    value_sum = jnp.zeros((KEYS, HEAD_SIZE), jnp.float32)
    products(0)
    for head in range(HEADS):
        if head + 1 < HEADS:
            products(head + 1)
        if head > 0:
            value_sum = finish(head - 1, value_sum)
        softmax(head)
    value_sum = finish(HEADS - 1, value_sum)
    sums[HEADS] = jnp.dot(
        value_low, value_sum.astype(jnp.bfloat16), preferred_element_type=jnp.float32
    )
    for head in range(HEADS + 1):
        even = sums[head, 0:32, :]
        odd = sums[head, 32:64, :]
        keep_ref[:, lanes(head)] = jnp.where(first, even, odd)
        send_ref[:, lanes(head)] = jnp.where(first, odd, even).astype(jnp.bfloat16)


def pair_kernel(place, keep_ref, got_ref, out_ref):
    rows = RANK // 2
    first = jnp.broadcast_to(place[0:1, :128] % 2 == 0, (rows, 128))
    first = jnp.concatenate([first] * (FEATURES // 128), axis=1)
    got = got_ref[...].astype(jnp.float32)
    total = keep_ref[...] + jnp.where(first, got[rows:], got[:rows])
    upper = jnp.concatenate([total[:, HALF:], jnp.zeros((32, 2 * HALF - FEATURES))], axis=1)
    both = jnp.stack([total[:, :HALF], upper], axis=1).astype(jnp.bfloat16)
    for seq in range(2):
        out_ref[:, seq] = both


def score_kernel(rows_ref, up_query, up_value, out_ref):
    pieces = []
    squares = []
    for b in range(2):
        row = jnp.sum(rows_ref[:, b].astype(jnp.float32), axis=0)
        row = jnp.concatenate([row[0:1], row[1:2, : FEATURES - HALF]], axis=1)
        squares.append(jnp.sum(row * row))
        total = up_value[...] * row[:, HEADS * HEAD_SIZE :]
        for k in range(HEADS):
            total = total + up_query[pl.ds(k, SHARE, stride=HEADS), :] * row[
                :, k * HEAD_SIZE : (k + 1) * HEAD_SIZE
            ]
        pieces.append(jnp.sum(total.T, axis=0, keepdims=True))
    lane = lax.broadcasted_iota(jnp.int32, (1, 128), 1)
    tail = jnp.where(lane == 0, squares[0], jnp.where(lane == 1, squares[1], 0.0))
    line = jnp.concatenate(pieces + [tail], axis=1)
    for i in range(out_ref.shape[0]):
        out_ref[i] = line


def relay_kernel(in_ref, out_ref):
    line = jnp.sum(in_ref[...], axis=0)
    for i in range(out_ref.shape[0]):
        out_ref[i] = line


def final_kernel(in_ref, ids_ref, out_ref):
    halves = [jnp.sum(in_ref[:, s], axis=0) for s in range(2)]
    count = 2 * SHARE
    rest = []
    for b in range(2):
        square = halves[0][:, count + b : count + b + 1]
        part = [half[:, b * SHARE : (b + 1) * SHARE] for half in halves]
        scores = jnp.concatenate(part, axis=1) / jnp.sqrt(square + 1e-06)
        rest.append(scores)
    slot = lax.broadcasted_iota(jnp.int32, (count, count), 0)
    chosen = jnp.where(slot == ids_ref[...], 1.0, 0.0).astype(jnp.bfloat16)
    left = jnp.concatenate(rest, axis=0)
    pieces = []
    for _ in range(3):
        piece = left.astype(jnp.bfloat16)
        left = left - piece.astype(jnp.float32)
        pieces.append(piece.astype(jnp.float32))
    pieces.append(jnp.zeros((2, count), jnp.float32))
    stack = jnp.concatenate(pieces, axis=0).astype(jnp.bfloat16)
    total = jnp.dot(stack, chosen, preferred_element_type=jnp.float32)
    out_ref[...] = total[0:2] + total[2:4] + total[4:6]


def call(kernel, made, specs, scratch=(), flops=0, out_specs=None):
    return pl.pallas_call(
        kernel,
        out_shape=[jax.ShapeDtypeStruct(*one) for one in made],
        in_specs=specs,
        out_specs=out_specs or [VMEM] * len(made),
        scratch_shapes=list(scratch),
        compiler_params=pltpu.CompilerParams(vmem_limit_bytes=32 * 2**20),
        cost_estimate=pl.CostEstimate(flops=flops, bytes_accessed=2**20, transcendentals=0),
    )


def body(
    queries, attention_keys, attention_values, cotangent, low_rank, seq_lengths,
    window_stops, query_ids, query_up_gradients, value_up_gradients,
):
    bf, f32 = jnp.bfloat16, jnp.float32
    three = jnp.concatenate([attention_keys[0], attention_values[0], low_rank[0]], axis=0)
    (pack,) = call(pack_kernel, [((PACK, HEAD_SIZE), bf)], [VMEM])(three)
    count = 64
    early = lax.ppermute(pack, CTX, [(i, i + 2) for i in range(count - 2)])
    apart = [(i, i + 1 + 2 * (i % 2)) for i in range(count) if i + 1 + 2 * (i % 2) < count]
    spot = jnp.stack([lax.axis_index(CTX), lax.axis_index("seq")]).astype(jnp.int32)
    spot = jnp.concatenate([spot, seq_lengths, window_stops])
    both = jnp.concatenate([queries[0], cotangent[0]], axis=0)
    later, both = lax.optimization_barrier((pack, both))
    far = lax.ppermute(later, CTX, apart)
    tile = (TOKENS, TOKENS)
    scored = [((HEADS, *tile), f32), ((HEADS, *tile), f32), ((HEADS, 8, TOKENS), f32)]
    scratch = [pltpu.VMEM(tile, f32), pltpu.VMEM((2, *tile), f32)]
    flops = 2 * 2 * HEADS * TOKENS * TOKENS * HEAD_SIZE
    row = ((TOKENS, HEADS * HEAD_SIZE), bf)
    *own, g, place = call(
        own_kernel, scored + [row, ((8, TOKENS), jnp.int32)],
        [VMEM] * 3, scratch, flops,
    )(spot.reshape(1, 6), both, pack)
    early, own[2] = lax.optimization_barrier((early, own[2]))
    other = lax.ppermute(early, "core", [(0, 1), (1, 0)])
    near = call(
        functools.partial(block_kernel, 2), scored, [VMEM] * 4, scratch, flops
    )(place, both, g, early)
    ready = [*own, *near]
    packs = [pack, early, other, far]
    fresh = KEYS - EARLY * TOKENS
    keep, send = call(
        functools.partial(attention_kernel, EARLY), [((RANK // 2, FEATURES), f32), ((RANK // 2, FEATURES), bf)],
        [VMEM] * (8 + 3 * EARLY),
        [
            pltpu.VMEM((fresh, HEAD_SIZE), bf),
            pltpu.VMEM((fresh, HEAD_SIZE), bf),
            pltpu.VMEM((HEAD_SIZE, KEYS), bf),
            pltpu.VMEM((RANK, KEYS), bf),
            pltpu.VMEM((fresh, TOKENS), f32),
            pltpu.VMEM((HEADS + 1, RANK, HEAD_SIZE), f32),
            pltpu.VMEM((2, fresh, TOKENS), f32),
            pltpu.VMEM((2, fresh, TOKENS), f32),
            pltpu.VMEM((2, KEYS, TOKENS), bf),
            pltpu.VMEM((2, KEYS, TOKENS), bf),
        ],
        flops=2 * 4 * HEADS * TOKENS * KEYS * HEAD_SIZE,
    )(place, both, g, three, *packs, *ready)
    got = lax.all_gather(send, "core", axis=0, tiled=True)
    (sums,) = call(pair_kernel, [((RANK // 2, 2, 2, HALF), bf)], [VMEM] * 3)(
        place, keep, got
    )
    sums = lax.all_to_all(sums.reshape(RANK, 2, HALF), ("z", "y", "seq"), 0, 0, tiled=True)
    up_query = query_up_gradients.reshape(SHARE * HEADS, HEAD_SIZE)
    up_value = value_up_gradients.reshape(SHARE, HEAD_SIZE)
    (lines,) = call(score_kernel, [((16, 1, LINE), f32)], [VMEM] * 3)(
        sums.reshape(RANK // 2, 2, 2, HALF), up_query, up_value
    )
    lines = lax.all_to_all(lines, ("z", "core"), 0, 0, tiled=True)
    (lines,) = call(relay_kernel, [((32, 1, LINE), f32)], [VMEM])(lines)
    lines = lax.all_to_all(lines, ("tp", "y", "seq"), 0, 0, tiled=True)
    (ranked,) = call(final_kernel, [((2, 2 * SHARE), f32)], [VMEM] * 2)(
        lines.reshape(16, 2, 1, LINE), query_ids.reshape(1, 2 * SHARE)
    )
    return ranked.T


def solution(mesh):
    fine = Mesh(mesh.devices.reshape(4, 8, 2, 4, 2), ("y", "z", "core", "tp", "seq"))
    split = P("seq", CTX, "tp")
    placed = (split, split, split, split, P("seq", CTX, None), P(), P(), P(), split, split)
    return jax.shard_map(body, mesh=fine, in_specs=placed, out_specs=P(), check_vma=False)
```
